128 devices in a mesh: cfg: 2 (over y_lo), seq: 8 (over z, y_hi), head: 8 (over x, core).
Axes of the slice: x: 4, y: 4 (y_hi: 2, y_lo: 2; y = y_hi * 2 + y_lo), z: 4, core: 2. Of those that a mesh axis runs over, the one named last changes fastest.
Arguments:
- queries: bfloat16 [2, 6144, 5120], P('cfg', 'seq', 'head'), may hold values from -8 to 8
- keys: bfloat16 [2, 6144, 5120], P('cfg', 'seq', 'head'), may hold values from -8 to 8
- values: bfloat16 [2, 6144, 5120], P('cfg', 'seq', 'head'), may hold values from -6 to 6
- hidden_in: bfloat16 [2, 6144, 5120], P('cfg', 'seq'), may hold values from -8 to 8
- out_weight: bfloat16 [5120, 5120], P('head'), may hold values from -0.125 to 0.125
- gate: float32 [5120], replicated, may hold values from 0.1 to 1.9
- mod_scale: float32 [5120], replicated, may hold values from 0.1 to 1.9
- mod_shift: float32 [5120], replicated, may hold values from -4 to 4
- head_weight: bfloat16 [5120, 64], replicated, may hold values from -0.015625 to 0.015625
- latent: float32 [6144, 64], P('seq', 'cfg'), may hold values from -6 to 6
- history: float32 [3, 6144, 64], P(None, 'seq', 'cfg'), may hold values from -16 to 16
- step_index: int32 [1], replicated, may hold values from 3 to 49
Outputs:
- guided: float32 [6144, 64], P('seq', 'cfg')
- latent_next: float32 [6144, 64], P('seq', 'cfg')
The draws below stay inside these ranges and needn't reach their ends.
All inputs are finite; a program needn't handle non-finite values.
Results may differ from the reference program's by a relative error of at most 0.0029.
Values may be sent and summed in bfloat16 or wider, within the bound.
No kernel may reach another device: no remote copies, remote signals or barrier semaphores. Data moves between devices by JAX's collectives and lax.ppermute only.
A program may use at most 256 MiB of HBM per device.

```python
import math
import jax
import jax.numpy as jnp
from jax import lax

D = 5120
HEADS = 40
HSIZE = 128
CH = 64
STEPS = 50
TOKENS = 6144


def draw_queries(key, part):
    key = jax.random.fold_in(key, 11)
    array_shape = (2, TOKENS, HEADS * HSIZE)
    return jnp.clip(1.5 * jax.random.normal(key, array_shape, jnp.float32), -8.0, 8.0).astype(jnp.bfloat16)


def draw_keys(key, part):
    key = jax.random.fold_in(key, 12)
    array_shape = (2, TOKENS, HEADS * HSIZE)
    return jnp.clip(1.5 * jax.random.normal(key, array_shape, jnp.float32), -8.0, 8.0).astype(jnp.bfloat16)


def draw_hidden_in(key, part):
    key = jax.random.fold_in(key, 13)
    first_key, second_key, third_key = jax.random.split(key, 3)
    array_shape = (2, TOKENS, D)
    column = jnp.arange(D).astype(jnp.float32)
    column_scale = 3.0 ** (column / D) * jnp.exp(jax.random.uniform(second_key, (D,), jnp.float32, -0.7, 0.7))
    row_scale = 0.3 * jnp.exp(jax.random.uniform(third_key, (2, TOKENS, 1), jnp.float32, 0.0, math.log(10.0)))
    sampled = jax.random.normal(first_key, array_shape, jnp.float32)
    return jnp.clip(0.5 * sampled * row_scale * column_scale, -8.0, 8.0).astype(jnp.bfloat16)


def spiked(drawn, key, source, target, shards_of, factor):
    owner, partner = [(jnp.arange(drawn.shape[dim]) // (drawn.shape[dim] // shards_of)).reshape([-1 if axis == dim else 1 for axis in range(drawn.ndim)]) for dim in (source, target)]
    chosen = jax.random.permutation(key, shards_of)[partner]
    strong = (owner == chosen) | (owner == (partner + shards_of // 2) % shards_of)
    return jnp.where(strong, factor * drawn, drawn)


def steps_of(own_key, dims, cuts, least, top_value):
    factor_of, own = 1.0, jax.random.fold_in(own_key, 6)
    for dim, parts in cuts:
        draws = jnp.exp(jax.random.uniform(jax.random.fold_in(own, dim), (parts,), jnp.float32, least / len(cuts), top_value / len(cuts)))
        factor_of = factor_of * jnp.repeat(draws, dims[dim] // parts).reshape([-1 if axis == dim else 1 for axis in range(len(dims))])
    return factor_of


def gaussian(key, dims, scale, most, shards=(), held_as=jnp.bfloat16):
    entries = jax.random.normal(key, dims, jnp.float32) * scale
    if len(shards) > 0:
        entries = steps_of(key, dims, shards, -0.22, 0.18) * entries
    return jnp.clip(entries, min=-most, max=most).astype(held_as)


def gaussian_with(own_key, dims, width, bound, pieces, heavy, kind=jnp.bfloat16):
    entries = width * jax.random.normal(own_key, dims, jnp.float32)
    if pieces:
        entries = entries * steps_of(own_key, dims, pieces, -0.22, 0.18)
    return jnp.clip(spiked(entries, jax.random.fold_in(own_key, 3), *heavy), -bound, bound).astype(kind)


def setup_inputs(seed: int = 0) -> dict:
    key_of = jax.random.split(jax.random.key(seed), 13)
    queries = draw_queries(jax.random.fold_in(key_of[12], 71), 0)
    keys = draw_keys(jax.random.fold_in(key_of[12], 71), 0)
    values = gaussian(key_of[2], (2, TOKENS, HEADS * HSIZE), 1.0, 6.0, ((0, 2), (1, 8), (2, 8)))
    hidden_in = draw_hidden_in(jax.random.fold_in(key_of[12], 71), 0)
    out_weight = gaussian_with(key_of[4], (HEADS * HSIZE, D), (HEADS * HSIZE) ** -0.5, 0.125, ((0, 8),), (0, 1, 8, 2.0))
    gate = jnp.clip(1.0 + 0.18 * jax.random.normal(key_of[5], (D,), jnp.float32), 0.1, 1.9)
    mod_scale = jnp.clip(1.0 + 0.18 * jax.random.normal(key_of[6], (D,), jnp.float32), 0.1, 1.9)
    mod_shift = gaussian(key_of[7], (D,), 1.0, 4.0, (), jnp.float32)
    head_weight = gaussian(key_of[8], (D, CH), (25 * D) ** -0.5, 0.015625)
    latent = gaussian(key_of[9], (TOKENS, CH), 1.0, 6.0, ((0, 8), (1, 2)), jnp.float32)
    history = gaussian(key_of[10], (3, TOKENS, CH), 3.0, 16.0, ((1, 8), (2, 2)), jnp.float32)
    step_index = jax.random.randint(key_of[11], (1,), 3, STEPS).astype(jnp.int32)
    return dict(queries=queries, keys=keys, values=values, hidden_in=hidden_in, out_weight=out_weight, gate=gate, mod_scale=mod_scale, mod_shift=mod_shift, head_weight=head_weight, latent=latent, history=history, step_index=step_index)


guide_scale = 5.0
flow_shift = 5.0
epsilon = 1e-06

def sigma_slope(step_number):
    moment = 1.0 - step_number.astype(jnp.float32) / STEPS
    return flow_shift / (1.0 + (flow_shift - 1.0) * moment) ** 2

def attend(operands):
    query_head, key_head, value_head = operands
    scores = jnp.dot(query_head, key_head.T, preferred_element_type=jnp.float32) * (1.0 / math.sqrt(HSIZE))
    row_peak = lax.optimization_barrier(jnp.max(scores, axis=1, keepdims=True))
    weights = jnp.exp(scores - row_peak)
    totals = lax.optimization_barrier(jnp.sum(weights, axis=1, keepdims=True))
    summed = jnp.dot(weights.astype(jnp.bfloat16), value_head, preferred_element_type=jnp.float32)
    return (summed / totals).astype(jnp.bfloat16)

def split_heads(matrix):
    return matrix.reshape(TOKENS, HEADS, HSIZE).transpose(1, 0, 2)

def branch_velocity(queries, keys, values, hidden_in, out_weight, gate, mod_scale, mod_shift, head_weight):
    attended = lax.map(attend, (split_heads(queries), split_heads(keys), split_heads(values)))
    attended = attended.transpose(1, 0, 2).reshape(TOKENS, HEADS * HSIZE)
    projected = jnp.dot(attended, out_weight, preferred_element_type=jnp.float32)
    residual = hidden_in.astype(jnp.float32) + gate * projected
    center = lax.optimization_barrier(jnp.mean(residual, axis=1, keepdims=True))
    spread = lax.optimization_barrier(jnp.mean(residual * residual, axis=1, keepdims=True)) - center * center
    normed = (residual - center) * lax.rsqrt(spread + epsilon) * mod_scale + mod_shift
    return jnp.dot(normed, head_weight.astype(jnp.float32), precision=lax.Precision.HIGHEST)

def reference(queries, keys, values, hidden_in, out_weight, gate, mod_scale, mod_shift, head_weight, latent, history, step_index):
    conditioned = branch_velocity(queries[0], keys[0], values[0], hidden_in[0], out_weight, gate, mod_scale, mod_shift, head_weight)
    unconditioned = branch_velocity(queries[1], keys[1], values[1], hidden_in[1], out_weight, gate, mod_scale, mod_shift, head_weight)
    guided = unconditioned + guide_scale * (conditioned - unconditioned)
    current_step = step_index[0]
    slopes = [sigma_slope(current_step - behind) for behind in range(4)]
    combined = (55.0 * slopes[0] * guided - 59.0 * slopes[1] * history[0] + 37.0 * slopes[2] * history[1] - 9.0 * slopes[3] * history[2]) / 24.0
    advanced = latent - combined / STEPS
    return (guided, advanced)
```

```python
import functools
import math

import jax
import jax.numpy as jnp
from jax import lax
from jax.experimental import pallas as pl
from jax.experimental.pallas import tpu as pltpu
from jax.sharding import PartitionSpec as P

HSIZE = 128
STEPS = 50

guide_scale = 5.0
flow_shift = 5.0
epsilon = 1e-06

Z, YH, X, CORE = 4, 2, 4, 2
SEQ, HEAD = Z * YH, X * CORE

z_groups = [[z * YH + y for z in range(Z)] for y in range(YH)]
y_swap = [(s, s ^ 1) for s in range(SEQ)]
core_swap = [(h, h ^ 1) for h in range(HEAD)]
cfg_swap = [(0, 1), (1, 0)]
transposition = [(s * HEAD + h, h * HEAD + s) for s in range(SEQ) for h in range(HEAD)]


def x_shift(step):
    return [(x * CORE + c, (x + step) % X * CORE + c) for x in range(X) for c in range(CORE)]


def sigma_slope(step_number):
    moment = 1.0 - step_number.astype(jnp.float32) / STEPS
    return flow_shift / (1.0 + (flow_shift - 1.0) * moment) ** 2


def attend_body(query_ref, *refs, parts, part, chunk):
    key_refs, value_refs = refs[:parts], refs[parts : 2 * parts]
    out_ref, keys_t, values_one = refs[2 * parts :]
    tokens = parts * part

    @pl.when(pl.program_id(0) == 0)
    def _():
        step = 384
        for index in range(parts):
            for at in range(0, part, step):
                block = key_refs[index][at : at + step, :].astype(jnp.float32)
                block = block.T.astype(jnp.bfloat16)
                start = index * part + at
                keys_t[:HSIZE, start : start + step] = block
                keys_t[HSIZE:, start : start + step] = block
            rows = slice(index * part, (index + 1) * part)
            values_one[rows, :HSIZE] = value_refs[index][...]
            values_one[rows, HSIZE:] = jnp.ones((part, HSIZE), jnp.bfloat16)

    scaled = query_ref[...].astype(jnp.float32) * (math.log2(math.e) / math.sqrt(HSIZE))
    upper = scaled.astype(jnp.bfloat16)
    lower = (scaled - upper.astype(jnp.float32)).astype(jnp.bfloat16)
    queries = jnp.concatenate([upper, lower], axis=1)

    def score(at):
        return jnp.dot(queries, keys_t[:, at : at + chunk], preferred_element_type=jnp.float32)

    peak, total = None, None
    scores = score(0)
    for at in range(0, tokens, chunk):
        following = score(at + chunk) if at + chunk < tokens else None
        new_peak = jnp.max(scores, axis=1, keepdims=True)
        if peak is not None:
            new_peak = jnp.maximum(peak, new_peak)
        weights = jnp.exp2(scores - new_peak).astype(jnp.bfloat16)
        summed = jnp.dot(
            weights, values_one[at : at + chunk, :], preferred_element_type=jnp.float32
        )
        total = summed if peak is None else total * jnp.exp2(peak - new_peak) + summed
        peak, scores = new_peak, following
    out_ref[...] = (total[:, :HSIZE] / total[:, HSIZE:]).astype(jnp.bfloat16)


def attend(queries, keys, values, rows, chunk):
    parts, part = len(keys), keys[0].shape[0]
    tokens = parts * part
    whole = pl.BlockSpec((part, HSIZE), lambda i: (0, 0))
    tile = pl.BlockSpec((rows, HSIZE), lambda i: (i, 0))
    return pl.pallas_call(
        functools.partial(attend_body, parts=parts, part=part, chunk=chunk),
        grid=(queries.shape[0] // rows,),
        in_specs=[tile] + [whole] * (2 * parts),
        out_specs=tile,
        out_shape=jax.ShapeDtypeStruct(queries.shape, jnp.bfloat16),
        scratch_shapes=[
            pltpu.VMEM((2 * HSIZE, tokens), jnp.bfloat16),
            pltpu.VMEM((tokens, 2 * HSIZE), jnp.bfloat16),
        ],
        compiler_params=pltpu.CompilerParams(vmem_limit_bytes=52 * 2**20),
        cost_estimate=pl.CostEstimate(
            flops=8 * queries.shape[0] * tokens * HSIZE,
            bytes_accessed=4 * HSIZE * (queries.shape[0] + tokens),
            transcendentals=queries.shape[0] * tokens,
        ),
    )(queries, *keys, *values)


def per_device(
    queries,
    keys,
    values,
    hidden_in,
    out_weight,
    gate,
    mod_scale,
    mod_shift,
    head_weight,
    latent,
    history,
    step_index,
):
    queries, keys, values, hidden = queries[0], keys[0], values[0], hidden_in[0]
    local_tokens, local_width = queries.shape
    full_width = hidden.shape[1]
    spread = Z * HSIZE
    core = lax.axis_index("head") % CORE
    column = lax.axis_index("head") // CORE
    branch = lax.axis_index("cfg")

    last = jnp.stack([keys[:, spread:], values[:, spread:], queries[:, spread:]])
    last = lax.ppermute(last, ("seq", "head"), transposition)
    last_gathered = lax.all_gather(last[:2], "head", axis=1, tiled=True)

    half = full_width // CORE
    own_weight = lax.dynamic_slice_in_dim(out_weight, core * half, half, 1)
    other_weight = lax.ppermute(
        lax.dynamic_slice_in_dim(out_weight, (1 - core) * half, half, 1), "head", core_swap
    )

    def deal(value):
        return lax.all_to_all(
            value[:, :spread], "seq", 1, 0, tiled=True, axis_index_groups=z_groups
        )

    own_keys = deal(keys)
    partner_keys = lax.ppermute(own_keys, "seq", y_swap)
    own_values = deal(values)
    partner_values = lax.ppermute(own_values, "seq", y_swap)
    dealt_queries = deal(queries)
    dealt = attend(
        dealt_queries, [own_keys, partner_keys], [own_values, partner_values], 768, 3072
    )
    last_out = attend(last[2], [last_gathered[0]], [last_gathered[1]], 768, 3072)
    returned = lax.all_to_all(dealt, "seq", 0, 1, tiled=True, axis_index_groups=z_groups)
    last_out = lax.ppermute(last_out, ("seq", "head"), transposition)
    attended = jnp.concatenate([returned, last_out], axis=1)

    other_attended = lax.ppermute(attended, "head", core_swap)
    partial = jnp.dot(attended, own_weight, preferred_element_type=jnp.float32) + jnp.dot(
        other_attended, other_weight, preferred_element_type=jnp.float32
    )

    share = local_tokens // X

    def quarter(step):
        return lax.dynamic_slice_in_dim(partial, (column + step) % X * share, share, 0)

    summed = quarter(0)
    for step in (1, 3, 2):
        arrived = lax.ppermute(quarter(step).astype(jnp.bfloat16), "head", x_shift(step))
        summed = summed + arrived.astype(jnp.float32)

    my_hidden = lax.dynamic_slice(hidden, (column * share, core * half), (share, half))

    def my_half(vector):
        return lax.dynamic_slice_in_dim(vector, core * half, half, 0)

    residual = my_hidden.astype(jnp.float32) + my_half(gate) * summed
    scaled_weight = my_half(head_weight).astype(jnp.float32)
    scale_part, shift_part = my_half(mod_scale), my_half(mod_shift)
    sums = jnp.stack([jnp.sum(residual, axis=1), jnp.sum(residual * residual, axis=1)], axis=1)
    other_sums = lax.ppermute(sums, "head", core_swap)
    sums = (sums + other_sums) / full_width
    center = sums[:, :1]
    inverse = lax.rsqrt(sums[:, 1:] - center * center + epsilon)
    normed = (residual - center) * inverse * scale_part + shift_part
    velocity = jnp.dot(normed, scaled_weight, precision=lax.Precision.HIGHEST)
    velocity = velocity + lax.ppermute(velocity, "head", core_swap)

    channels = velocity.shape[1] // 2
    outgoing = lax.dynamic_slice_in_dim(velocity, (1 - branch) * channels, channels, 1)
    partner_velocity = lax.ppermute(outgoing, "cfg", cfg_swap)
    own_velocity = lax.dynamic_slice_in_dim(velocity, branch * channels, channels, 1)
    conditioned = jnp.where(branch == 0, own_velocity, partner_velocity)
    unconditioned = jnp.where(branch == 0, partner_velocity, own_velocity)
    guided = unconditioned + guide_scale * (conditioned - unconditioned)
    x_groups = [[x * CORE + c for x in range(X)] for c in range(CORE)]
    guided = lax.all_to_all(
        jnp.broadcast_to(guided[None], (X, share, channels)),
        "head",
        0,
        0,
        tiled=True,
        axis_index_groups=x_groups,
    ).reshape(local_tokens, channels)

    current_step = step_index[0]
    slopes = [sigma_slope(current_step - behind) for behind in range(4)]
    combined = (
        55.0 * slopes[0] * guided
        - 59.0 * slopes[1] * history[0]
        + 37.0 * slopes[2] * history[1]
        - 9.0 * slopes[3] * history[2]
    ) / 24.0
    advanced = latent - combined / STEPS
    return (guided, advanced)


def solution(mesh):
    placed = (
        P("cfg", "seq", "head"),
        P("cfg", "seq", "head"),
        P("cfg", "seq", "head"),
        P("cfg", "seq", None),
        P("head", None),
        P(),
        P(),
        P(),
        P(),
        P("seq", "cfg"),
        P(None, "seq", "cfg"),
        P(),
    )
    return jax.shard_map(
        per_device,
        mesh=mesh,
        in_specs=placed,
        out_specs=(P("seq", "cfg"), P("seq", "cfg")),
        check_vma=False,
    )
```

```python
import functools
import math

import jax
import jax.numpy as jnp
from jax import lax
from jax.experimental import pallas as pl
from jax.experimental.pallas import tpu as pltpu
from jax.sharding import PartitionSpec as P

HSIZE = 128
STEPS = 50

guide_scale = 5.0
flow_shift = 5.0
epsilon = 1e-06

Z, YH, X, CORE = 4, 2, 4, 2
SEQ, HEAD = Z * YH, X * CORE

z_groups = [[z * YH + y for z in range(Z)] for y in range(YH)]
y_swap = [(s, s ^ 1) for s in range(SEQ)]
core_swap = [(h, h ^ 1) for h in range(HEAD)]
cfg_swap = [(0, 1), (1, 0)]


def x_shift(step):
    return [(x * CORE + c, (x + step) % X * CORE + c) for x in range(X) for c in range(CORE)]


def sigma_slope(step_number):
    moment = 1.0 - step_number.astype(jnp.float32) / STEPS
    return flow_shift / (1.0 + (flow_shift - 1.0) * moment) ** 2


def attend_body(*refs, begun, ended, rows, subs, chunk):
    query_ref, key_ref, value_ref = refs[:3]
    refs = refs[3:]
    if begun:
        sum_in, stat_in = refs[:2]
        refs = refs[2:]
    if ended:
        out_ref = refs[0]
        refs = refs[1:]
    else:
        sum_out, stat_out = refs[:2]
        refs = refs[2:]
    keys_t, values_one = refs
    tokens = key_ref.shape[0]

    @pl.when(pl.program_id(0) == 0)
    def _():
        step = 384
        for at in range(0, tokens, step):
            block = key_ref[at : at + step, :].astype(jnp.float32).T.astype(jnp.bfloat16)
            keys_t[:HSIZE, at : at + step] = block
            keys_t[HSIZE:, at : at + step] = block
        values_one[:, :HSIZE] = value_ref[...]
        values_one[:, HSIZE:] = jnp.ones((tokens, HSIZE), jnp.bfloat16)

    work = [(sub, at) for sub in range(subs) for at in range(0, tokens, chunk)]

    def score(item):
        sub, at = item
        scaled = query_ref[sub * rows : (sub + 1) * rows, :].astype(jnp.float32)
        scaled = scaled * (math.log2(math.e) / math.sqrt(HSIZE))
        upper = scaled.astype(jnp.bfloat16)
        lower = (scaled - upper.astype(jnp.float32)).astype(jnp.bfloat16)
        return jnp.dot(
            jnp.concatenate([upper, lower], axis=1),
            keys_t[:, at : at + chunk],
            preferred_element_type=jnp.float32,
        )

    peak, total = None, None
    scores = score(work[0])
    for index, (sub, at) in enumerate(work):
        following = score(work[index + 1]) if index + 1 < len(work) else None
        new_peak = jnp.max(scores, axis=1, keepdims=True)
        if at > 0:
            new_peak = jnp.maximum(peak, new_peak)
        weights = jnp.exp2(scores - new_peak).astype(jnp.bfloat16)
        summed = jnp.dot(weights, values_one[at : at + chunk, :], preferred_element_type=jnp.float32)
        total = summed if at == 0 else total * jnp.exp2(peak - new_peak) + summed
        peak, scores = new_peak, following
        if at + chunk == tokens:
            span = slice(sub * rows, (sub + 1) * rows)
            top, low = total[:, :HSIZE], total[:, HSIZE:]
            if begun:
                peak_in, low_in = stat_in[span, :1], stat_in[span, 1:2]
                both = jnp.maximum(peak, peak_in)
                here, there = jnp.exp2(peak - both), jnp.exp2(peak_in - both)
                top = top * here + sum_in[span, :] * there
                low = low * here + low_in * there
                peak = both
            if ended:
                out_ref[span, :] = (top / low).astype(jnp.bfloat16)
            else:
                lane = lax.broadcasted_iota(jnp.int32, low.shape, 1)
                sum_out[span, :] = top
                stat_out[span, :] = jnp.where(lane == 0, peak, low)

def attend(queries, keys, values, state=None, last=True, rows=768, subs=1, chunk=1536):
    count, tokens = queries.shape[0], keys.shape[0]
    tile = pl.BlockSpec((rows * subs, HSIZE), lambda i: (i, 0))
    whole = pl.BlockSpec((tokens, HSIZE), lambda i: (0, 0))
    wide = jax.ShapeDtypeStruct((count, HSIZE), jnp.float32)
    return pl.pallas_call(
        functools.partial(attend_body, begun=state is not None, ended=last, rows=rows, subs=subs, chunk=chunk),
        grid=(count // (rows * subs),),
        in_specs=[tile, whole, whole] + ([] if state is None else [tile, tile]),
        out_specs=tile if last else [tile, tile],
        out_shape=jax.ShapeDtypeStruct((count, HSIZE), jnp.bfloat16) if last else [wide, wide],
        scratch_shapes=[
            pltpu.VMEM((2 * HSIZE, tokens), jnp.bfloat16),
            pltpu.VMEM((tokens, 2 * HSIZE), jnp.bfloat16),
        ],
        compiler_params=pltpu.CompilerParams(vmem_limit_bytes=56 * 2**20),
        cost_estimate=pl.CostEstimate(
            flops=8 * count * tokens * HSIZE,
            bytes_accessed=4 * HSIZE * (count + tokens),
            transcendentals=count * tokens,
        ),
    )(queries, keys, values, *(state or ()))


def per_device(
    queries,
    keys,
    values,
    hidden_in,
    out_weight,
    gate,
    mod_scale,
    mod_shift,
    head_weight,
    latent,
    history,
    step_index,
):
    queries, keys, values, hidden = queries[0], keys[0], values[0], hidden_in[0]
    local_tokens = queries.shape[0]
    full_width = hidden.shape[1]
    spread = Z * HSIZE
    half, share = full_width // CORE, local_tokens // X
    core = lax.axis_index("head") % CORE
    column = lax.axis_index("head") // CORE
    branch = lax.axis_index("cfg")

    fifth = lax.all_gather(
        jnp.stack([keys[:, spread:], values[:, spread:]]), "seq", axis=1, tiled=True
    )

    weight = lax.dynamic_slice_in_dim(out_weight, core * half, half, 1)
    other_weight = lax.dynamic_slice_in_dim(out_weight, (1 - core) * half, half, 1)
    weight = jnp.concatenate([weight, lax.ppermute(other_weight, "head", core_swap)])

    def deal(value):
        blocks = value[:, :spread].reshape(local_tokens, Z, HSIZE).transpose(1, 0, 2)
        return lax.all_to_all(
            blocks, "seq", 0, 0, tiled=True, axis_index_groups=z_groups
        ).reshape(Z * local_tokens, HSIZE)

    own_keys = deal(keys)
    partner_keys = lax.ppermute(own_keys, "seq", y_swap)
    values, own_keys = lax.optimization_barrier((values, own_keys))
    own_values = deal(values)
    partner_values = lax.ppermute(own_values, "seq", y_swap)
    dealt_queries, own_values = lax.optimization_barrier((queries, own_values))
    dealt_queries = deal(dealt_queries)
    dealt_queries, weight = lax.optimization_barrier((dealt_queries, weight))

    state = attend(dealt_queries, own_keys, own_values, None, False, 768, 2, 3072)
    dealt = attend(dealt_queries, partner_keys, partner_values, state, True, 768, 2, 3072)
    fifth_queries, dealt = lax.optimization_barrier((queries[:, spread:], dealt))
    dealt = lax.all_to_all(
        dealt.reshape(Z, local_tokens, HSIZE), "seq", 0, 0, tiled=True, axis_index_groups=z_groups
    )
    fifth_out = attend(fifth_queries, fifth[0], fifth[1], None, True, 768, 1, 3072)
    attended = jnp.concatenate(
        [dealt.transpose(1, 0, 2).reshape(local_tokens, spread), fifth_out], axis=1
    )
    attended = jnp.concatenate([attended, lax.ppermute(attended, "head", core_swap)], axis=1)

    def quarter(step):
        rows = lax.dynamic_slice_in_dim(attended, (column + step) % X * share, share, 0)
        return jnp.dot(rows, weight, preferred_element_type=jnp.float32)

    wire, middle = jnp.bfloat16, share // 2
    opposite = quarter(2).astype(wire)
    behind_far = lax.ppermute(opposite[:middle], "head", x_shift(1))
    ahead_far = lax.ppermute(opposite[middle:], "head", x_shift(3))
    forward, backward = quarter(1), quarter(3)
    forward = jnp.concatenate(
        [forward[:middle] + behind_far.astype(jnp.float32), forward[middle:]]
    ).astype(wire)
    backward = jnp.concatenate(
        [backward[:middle], backward[middle:] + ahead_far.astype(jnp.float32)]
    ).astype(wire)
    behind = lax.ppermute(forward, "head", x_shift(1))
    ahead = lax.ppermute(backward, "head", x_shift(3))
    summed = quarter(0) + behind.astype(jnp.float32) + ahead.astype(jnp.float32)

    my_hidden = lax.dynamic_slice(hidden, (column * share, core * half), (share, half))

    def my_half(vector):
        return lax.dynamic_slice_in_dim(vector, core * half, half, 0)

    residual = my_hidden.astype(jnp.float32) + my_half(gate) * summed
    weight_part = my_half(head_weight).astype(jnp.float32)
    scale_part, shift_part = my_half(mod_scale), my_half(mod_shift)
    projected = jnp.dot(residual * scale_part, weight_part, precision=lax.Precision.HIGHEST)
    levels = jnp.dot(
        jnp.stack([scale_part, shift_part]), weight_part, precision=lax.Precision.HIGHEST
    )
    levels = levels + lax.ppermute(levels, "head", core_swap)
    channels = projected.shape[1] // 2
    sums = jnp.stack([jnp.sum(residual, axis=1), jnp.sum(residual * residual, axis=1)], axis=1)
    parts = jnp.concatenate([projected, sums], axis=1)
    parts = parts + lax.ppermute(parts, "head", core_swap)
    center = parts[:, 2 * channels : 2 * channels + 1] / full_width
    inverse = lax.rsqrt(parts[:, 2 * channels + 1 :] / full_width - center * center + epsilon)
    velocity = (parts[:, : 2 * channels] - center * levels[:1]) * inverse + levels[1:]

    outgoing = lax.dynamic_slice_in_dim(velocity, (1 - branch) * channels, channels, 1)
    partner_velocity = lax.ppermute(outgoing, "cfg", cfg_swap)
    own_velocity = lax.dynamic_slice_in_dim(velocity, branch * channels, channels, 1)
    conditioned = jnp.where(branch == 0, own_velocity, partner_velocity)
    unconditioned = jnp.where(branch == 0, partner_velocity, own_velocity)
    guided = unconditioned + guide_scale * (conditioned - unconditioned)
    ring = [guided] + [lax.ppermute(guided, "head", x_shift(X - ahead)) for ahead in range(1, X)]
    guided = lax.dynamic_slice_in_dim(
        jnp.concatenate(ring + ring[:-1]), (X - column) % X * share, local_tokens, 0
    )

    current_step = step_index[0]
    slopes = [sigma_slope(current_step - behind) for behind in range(4)]
    combined = (
        55.0 * slopes[0] * guided
        - 59.0 * slopes[1] * history[0]
        + 37.0 * slopes[2] * history[1]
        - 9.0 * slopes[3] * history[2]
    ) / 24.0
    advanced = latent - combined / STEPS
    return (guided, advanced)


def solution(mesh):
    placed = (
        P("cfg", "seq", "head"),
        P("cfg", "seq", "head"),
        P("cfg", "seq", "head"),
        P("cfg", "seq", None),
        P("head", None),
        P(),
        P(),
        P(),
        P(),
        P("seq", "cfg"),
        P(None, "seq", "cfg"),
        P(),
    )
    return jax.shard_map(
        per_device,
        mesh=mesh,
        in_specs=placed,
        out_specs=(P("seq", "cfg"), P("seq", "cfg")),
        check_vma=False,
    )
```

```python
import functools
import math

import jax
import jax.numpy as jnp
from jax import lax
from jax.experimental import pallas as pl
from jax.experimental.pallas import tpu as pltpu
from jax.sharding import PartitionSpec as P

HSIZE = 128
STEPS = 50
SUMS = 8

guide_scale = 5.0
flow_shift = 5.0
epsilon = 1e-06

Z, YH, X, CORE = 4, 2, 4, 2
SEQ, HEAD = Z * YH, X * CORE

z_groups = [[z * YH + y for z in range(Z)] for y in range(YH)]
core_swap = [(h, h ^ 1) for h in range(HEAD)]
cfg_swap = [(0, 1), (1, 0)]
both_swap = [(n, n ^ (HEAD + 1)) for n in range(2 * HEAD)]


def traded(step, flip=0):
    return [
        (
            (z * YH + y) * HEAD + x * CORE + c,
            ((z + step) % Z * YH + c) * HEAD + x * CORE + (y + flip) % CORE,
        )
        for z in range(Z)
        for y in range(YH)
        for x in range(X)
        for c in range(CORE)
    ]


def x_shift(step):
    return [(x * CORE + c, (x + step) % X * CORE + c) for x in range(X) for c in range(CORE)]


def sigma_slope(step_number):
    moment = 1.0 - step_number.astype(jnp.float32) / STEPS
    return flow_shift / (1.0 + (flow_shift - 1.0) * moment) ** 2


def pack_body(place, *refs, heads):
    sources, outs = refs[:3], refs[3:]
    number = 0
    for out, count in zip(outs, heads):
        for head in range(count):

            @pl.when(pl.program_id(0) == number)
            def _(out=out, head=head):
                for kind, source in enumerate(sources):
                    out[3 * head + kind] = source[...]

            number += 1


def pack(place, sources, steps, heads):
    tokens = sources[0].shape[0]

    def column(i, place):
        step = sum(jnp.where(i == n, step, 0) for n, step in enumerate(steps))
        return 0, jnp.where(i < len(steps), (place[3] + step) % Z, Z)

    return pl.pallas_call(
        functools.partial(pack_body, heads=heads),
        grid_spec=pltpu.PrefetchScalarGridSpec(
            num_scalar_prefetch=1,
            grid=(sum(heads),),
            in_specs=[pl.BlockSpec((tokens, HSIZE), column)] * len(sources),
            out_specs=[
                pl.BlockSpec((3 * count, tokens, HSIZE), lambda i, place: (0, 0, 0))
                for count in heads
            ],
        ),
        out_shape=[
            jax.ShapeDtypeStruct((3 * count, tokens, HSIZE), jnp.bfloat16) for count in heads
        ],
        compiler_params=pltpu.CompilerParams(vmem_limit_bytes=56 * 2**20),
    )(place, *sources)


def attend_body(*refs, heads, parts, chunk):
    query_refs, refs = refs[:heads], refs[heads:]
    key_refs, value_refs, refs = refs[:parts], refs[parts : 2 * parts], refs[2 * parts :]
    out_refs, (query_ref, keys_t, values_one) = refs[:heads], refs[heads:]
    tokens = values_one.shape[0]

    for index in range(heads):

        @pl.when(pl.program_id(0) == index)
        def _(ref=query_refs[index]):
            query_ref[...] = ref[...]

    @pl.when(pl.program_id(0) == 0)
    def _():
        step, start = 384, 0
        for key_ref, value_ref in zip(key_refs, value_refs):
            length = key_ref.shape[0]
            for at in range(0, length, step):
                block = key_ref[at : at + step, :].astype(jnp.float32).T.astype(jnp.bfloat16)
                keys_t[:HSIZE, start + at : start + at + step] = block
                keys_t[HSIZE:, start + at : start + at + step] = block
            values_one[start : start + length, :HSIZE] = value_ref[...]
            start += length
        values_one[:, HSIZE:] = jnp.ones((tokens, HSIZE), jnp.bfloat16)

    scaled = query_ref[...].astype(jnp.float32) * (math.log2(math.e) / math.sqrt(HSIZE))
    upper = scaled.astype(jnp.bfloat16)
    lower = (scaled - upper.astype(jnp.float32)).astype(jnp.bfloat16)
    queries = jnp.concatenate([upper, lower], axis=1)

    def score(at):
        return jnp.dot(queries, keys_t[:, at : at + chunk], preferred_element_type=jnp.float32)

    peak, total = None, None
    scores = score(0)
    for at in range(0, tokens, chunk):
        following = score(at + chunk) if at + chunk < tokens else None
        new_peak = jnp.max(scores, axis=1, keepdims=True)
        if at > 0:
            new_peak = jnp.maximum(peak, new_peak)
        weights = jnp.exp2(scores - new_peak).astype(jnp.bfloat16)
        summed = jnp.dot(
            weights, values_one[at : at + chunk, :], preferred_element_type=jnp.float32
        )
        total = summed if at == 0 else total * jnp.exp2(peak - new_peak) + summed
        peak, scores = new_peak, following
    result = (total[:, :HSIZE] / total[:, HSIZE:]).astype(jnp.bfloat16)
    for index in range(heads):

        @pl.when(pl.program_id(0) == index)
        def _(ref=out_refs[index]):
            ref[...] = result


def attend(queries, keys, values, chunk=3072):
    rows = queries[0][0].shape[1]
    tokens = sum(part.shape[1] for part, _ in keys)
    operands = (*queries, *keys, *values)
    return pl.pallas_call(
        functools.partial(attend_body, heads=len(queries), parts=len(keys), chunk=chunk),
        grid=(len(queries),),
        in_specs=[
            pl.BlockSpec((pl.squeezed, array.shape[1], HSIZE), lambda i, index=index: (index, 0, 0))
            for array, index in operands
        ],
        out_specs=[pl.BlockSpec((rows, HSIZE), lambda i: (0, 0))] * len(queries),
        out_shape=[jax.ShapeDtypeStruct((rows, HSIZE), jnp.bfloat16)] * len(queries),
        scratch_shapes=[
            pltpu.VMEM((rows, HSIZE), jnp.bfloat16),
            pltpu.VMEM((2 * HSIZE, tokens), jnp.bfloat16),
            pltpu.VMEM((tokens, 2 * HSIZE), jnp.bfloat16),
        ],
        compiler_params=pltpu.CompilerParams(vmem_limit_bytes=56 * 2**20),
        cost_estimate=pl.CostEstimate(flops=1000, bytes_accessed=1000, transcendentals=0),
    )(*(array for array, _ in operands))


def project_body(place, *refs, steps):
    operands, own_weight, other_weight, outs = refs[: 2 * Z + 2], *refs[2 * Z + 2 :][:2], refs[2 * Z + 4 : -2]
    rows, weight = refs[-2:]
    share = rows.shape[0] // len(steps)
    depth = own_weight.shape[0]

    @pl.when(pl.program_id(0) == 0)
    def _():
        for index, step in enumerate(steps):
            start = pl.multiple_of((place[0] + step) % X * share, share)
            span = slice(index * share, (index + 1) * share)
            for number, ref in enumerate(operands):
                side, head = divmod(number, Z + 1)
                at = side * depth + (spread(place, head) if head < Z else Z * HSIZE)
                rows[span, pl.ds(at, HSIZE)] = ref[pl.ds(start, share), :]

    weight[:depth] = own_weight[...]
    weight[depth:] = other_weight[...]
    product = jnp.dot(rows[...], weight[...], preferred_element_type=jnp.float32)
    height = outs[0].shape[0]
    for index, out in enumerate(outs):
        out[...] = product[index * height : (index + 1) * height].astype(out.dtype)


def spread(place, step):
    return pl.multiple_of((place[3] + step) % Z * HSIZE, HSIZE)


def project(place, attended, own_weight, other_weight, steps, kinds, height, tile=1280):
    depth, half = other_weight.shape
    rows = attended[0].shape[0] // X * len(steps)
    tiles = half // tile
    return pl.pallas_call(
        functools.partial(project_body, steps=steps),
        grid_spec=pltpu.PrefetchScalarGridSpec(
            num_scalar_prefetch=1,
            grid=(tiles,),
            in_specs=[
                pl.BlockSpec(operand.shape, lambda i, place: (0, 0)) for operand in attended
            ]
            + [
                pl.BlockSpec((depth, tile), lambda i, place: (0, place[1] * tiles + i)),
                pl.BlockSpec((depth, tile), lambda i, place: (0, i)),
            ],
            out_specs=[pl.BlockSpec((height, tile), lambda i, place: (0, i))] * len(kinds),
            scratch_shapes=[
                pltpu.VMEM((rows, 2 * depth), jnp.bfloat16),
                pltpu.VMEM((2 * depth, tile), jnp.bfloat16),
            ],
        ),
        out_shape=[jax.ShapeDtypeStruct((height, half), kind) for kind in kinds],
        compiler_params=pltpu.CompilerParams(vmem_limit_bytes=56 * 2**20),
        cost_estimate=pl.CostEstimate(flops=1000, bytes_accessed=1000, transcendentals=0),
    )(place, *attended, own_weight, other_weight)


def finish_body(place, *refs):
    own, arrived, hidden, gate, scale, head_weight = refs[:2], refs[2:6], *refs[6:10]
    kept, given, total, turned = refs[10:]
    index = pl.program_id(0)
    summed = [
        own[n][...] + arrived[n][...].astype(jnp.float32) + arrived[2 + n][...].astype(jnp.float32)
        for n in range(2)
    ]
    residual = hidden[...].astype(jnp.float32) + gate[...] * jnp.concatenate(summed, axis=0)
    rest = residual * scale[...]
    projected = None
    for _ in range(3):
        part = rest.astype(jnp.bfloat16)
        rest = rest - part.astype(jnp.float32)
        product = jnp.dot(part, head_weight[...], preferred_element_type=jnp.float32)
        projected = product if projected is None else projected + product
    channels = projected.shape[1]
    plain = jnp.sum(residual, axis=1, keepdims=True)
    square = jnp.sum(residual * residual, axis=1, keepdims=True)
    lane = lax.broadcasted_iota(jnp.int32, (residual.shape[0], HSIZE - channels), 1)
    sums = jnp.where(lane == 0, plain, jnp.where(lane == 1, square, 0.0))
    parts = jnp.concatenate([projected, sums], axis=1)

    @pl.when(index == 0)
    def _():
        total[...] = parts

    @pl.when(index > 0)
    def _():
        total[...] += parts

    @pl.when(index == pl.num_programs(0) - 1)
    def _():
        turned[...] = total[...].T
        part = channels // 2
        for out, branch in ((kept, place[2]), (given, 1 - place[2])):
            out[:part] = turned[pl.ds(pl.multiple_of(branch * part, part), part), :]
            out[part:] = turned[channels : channels + out.shape[0] - part, :]


def finish(place, own, arrived, hidden, gate, scale, head_weight, tile=1280):
    middle, half = own[0].shape
    share, tiles = 2 * middle, half // tile
    height = head_weight.shape[1] // 2 + SUMS
    block = pl.BlockSpec((middle, tile), lambda i, place: (0, i))
    vector = pl.BlockSpec((1, tile), lambda i, place: (0, place[1] * tiles + i))
    return pl.pallas_call(
        finish_body,
        grid_spec=pltpu.PrefetchScalarGridSpec(
            num_scalar_prefetch=1,
            grid=(tiles,),
            in_specs=[block] * 6
            + [
                pl.BlockSpec((share, tile), lambda i, place: (place[0], place[1] * tiles + i)),
                vector,
                vector,
                pl.BlockSpec(
                    (tile, head_weight.shape[1]), lambda i, place: (place[1] * tiles + i, 0)
                ),
            ],
            out_specs=[pl.BlockSpec((height, share), lambda i, place: (0, 0))] * 2,
            scratch_shapes=[
                pltpu.VMEM((share, HSIZE), jnp.float32),
                pltpu.VMEM((HSIZE, share), jnp.float32),
            ],
        ),
        out_shape=[jax.ShapeDtypeStruct((height, share), jnp.float32)] * 2,
        compiler_params=pltpu.CompilerParams(vmem_limit_bytes=56 * 2**20),
        cost_estimate=pl.CostEstimate(
            flops=6 * share * half * HSIZE, bytes_accessed=12 * share * half, transcendentals=0
        ),
    )(place, *own, *arrived, hidden, gate[None], scale[None], head_weight)


def per_device(
    queries,
    keys,
    values,
    hidden_in,
    out_weight,
    gate,
    mod_scale,
    mod_shift,
    head_weight,
    latent,
    history,
    step_index,
):
    queries, keys, values, hidden = queries[0], keys[0], values[0], hidden_in[0]
    local_tokens = queries.shape[0]
    full_width = hidden.shape[1]
    half, share = full_width // CORE, local_tokens // X
    core = lax.axis_index("head") % CORE
    column = lax.axis_index("head") // CORE
    branch = lax.axis_index("cfg")

    z = lax.axis_index("seq") // YH
    place = jnp.stack([column, core, branch, z]).astype(jnp.int32)
    pair = "seq", "head"

    order = (1, 3, 2, 0)
    messages = pack(place, (queries, keys, values), order, (1, 1, 1, 2))
    messages, weight = lax.optimization_barrier((messages, out_weight))
    near = {
        step: lax.ppermute(message, pair, traded(step)) for step, message in zip(order, messages)
    }
    other_weight = lax.ppermute(
        lax.dynamic_slice_in_dim(weight, (1 - core) * half, half, 1), "head", core_swap
    )
    far = {step: lax.ppermute(near[step][:3], "head", core_swap) for step in order}
    near, far, other_weight = lax.optimization_barrier((near, far, other_weight))
    fifth_near = lax.all_gather(
        near[0][4:], "seq", axis=1, tiled=True, axis_index_groups=z_groups
    )
    dealt = attend(
        [(near[step], 0) for step in order],
        [(side[step], 1) for side in (near, far) for step in order],
        [(side[step], 2) for side in (near, far) for step in order],
    )
    fifth_near, dealt = lax.optimization_barrier((fifth_near, dealt))
    fifth_far = lax.ppermute(fifth_near, "head", core_swap)
    back = {
        step: lax.ppermute(result, pair, traded(-step)) for step, result in zip(order, dealt)
    }
    (fifth_out,) = attend(
        [(near[0], 3)],
        [(fifth_near, 0), (fifth_far, 0)],
        [(fifth_near, 1), (fifth_far, 1)],
    )
    back, fifth_out = lax.optimization_barrier((back, fifth_out))
    own_attended = [back[step] for step in range(Z)]
    attended = (
        *own_attended,
        lax.ppermute(fifth_out, pair, traded(0)),
        *(lax.ppermute(part, "head", core_swap) for part in own_attended),
        lax.ppermute(fifth_out, pair, traded(0, 1)),
    )

    wire, middle = jnp.bfloat16, share // 2
    weights = out_weight, other_weight
    opposite = project(place, attended, *weights, (2,), (wire,) * 2, middle)
    behind_far = lax.ppermute(opposite[0], "head", x_shift(1))
    ahead_far = lax.ppermute(opposite[1], "head", x_shift(3))
    attended, opposite = lax.optimization_barrier((attended, opposite))
    *rest, own_upper, own_lower = project(
        place, attended, *weights, (1, 3, 0), (jnp.float32, wire, wire) + (jnp.float32,) * 3, middle
    )
    forward, forward_lower, backward_upper, backward = rest
    behind_lower = lax.ppermute(forward_lower, "head", x_shift(1))
    ahead_upper = lax.ppermute(backward_upper, "head", x_shift(3))
    forward = (forward + behind_far.astype(jnp.float32)).astype(wire)
    backward = (backward + ahead_far.astype(jnp.float32)).astype(wire)
    behind_upper = lax.ppermute(forward, "head", x_shift(1))
    ahead_lower = lax.ppermute(backward, "head", x_shift(3))
    arrived = behind_upper, behind_lower, ahead_upper, ahead_lower

    kept, given = finish(
        place, (own_upper, own_lower), arrived, hidden, gate, mod_scale, head_weight
    )
    here = kept + lax.ppermute(kept, "head", core_swap)
    there = lax.ppermute(given, "cfg", cfg_swap) + lax.ppermute(
        given, ("cfg", "head"), both_swap
    )
    channels = head_weight.shape[1] // 2
    levels = jnp.dot(
        head_weight.astype(jnp.float32).T,
        jnp.stack([mod_scale, mod_shift], axis=1),
        precision=lax.Precision.HIGHEST,
    )
    levels = lax.dynamic_slice_in_dim(levels, branch * channels, channels, 0)

    def velocity(total):
        center = total[channels : channels + 1] / full_width
        inverse = lax.rsqrt(total[channels + 1 : channels + 2] / full_width - center * center + epsilon)
        return (total[:channels] - center * levels[:, :1]) * inverse + levels[:, 1:]

    conditioned = velocity(jnp.where(branch == 0, here, there))
    unconditioned = velocity(jnp.where(branch == 0, there, here))
    guided = unconditioned + guide_scale * (conditioned - unconditioned)
    ring = [guided] + [lax.ppermute(guided, "head", x_shift(X - ahead)) for ahead in range(1, X)]
    guided = lax.dynamic_slice_in_dim(
        jnp.concatenate(ring + ring[:-1], axis=1), (X - column) % X * share, local_tokens, 1
    ).T

    current_step = step_index[0]
    slopes = [sigma_slope(current_step - behind) for behind in range(4)]
    combined = (
        55.0 * slopes[0] * guided
        - 59.0 * slopes[1] * history[0]
        + 37.0 * slopes[2] * history[1]
        - 9.0 * slopes[3] * history[2]
    ) / 24.0
    advanced = latent - combined / STEPS
    return (guided, advanced)


def solution(mesh):
    placed = (
        P("cfg", "seq", "head"),
        P("cfg", "seq", "head"),
        P("cfg", "seq", "head"),
        P("cfg", "seq", None),
        P("head", None),
        P(),
        P(),
        P(),
        P(),
        P("seq", "cfg"),
        P(None, "seq", "cfg"),
        P(),
    )
    return jax.shard_map(
        per_device,
        mesh=mesh,
        in_specs=placed,
        out_specs=(P("seq", "cfg"), P("seq", "cfg")),
        check_vma=False,
    )
```

```python
import functools
import math

import jax
import jax.numpy as jnp
from jax import lax
from jax.experimental import pallas as pl
from jax.experimental.pallas import tpu as pltpu
from jax.sharding import PartitionSpec as P

HSIZE = 128
STEPS = 50
SUMS = 8

guide_scale = 5.0
flow_shift = 5.0
epsilon = 1e-06

Z, YH, X, CORE = 4, 2, 4, 2
SEQ, HEAD = Z * YH, X * CORE

z_groups = [[z * YH + y for z in range(Z)] for y in range(YH)]
core_swap = [(h, h ^ 1) for h in range(HEAD)]
cfg_swap = [(0, 1), (1, 0)]
both_swap = [(n, n ^ (HEAD + 1)) for n in range(2 * HEAD)]


def traded(step):
    return [
        ((z * YH + y) * HEAD + x * CORE + c, ((z + step) % Z * YH + c) * HEAD + x * CORE + y)
        for z in range(Z)
        for y in range(YH)
        for x in range(X)
        for c in range(CORE)
    ]


def x_shift(step):
    return [(x * CORE + c, (x + step) % X * CORE + c) for x in range(X) for c in range(CORE)]


def sigma_slope(step_number):
    moment = 1.0 - step_number.astype(jnp.float32) / STEPS
    return flow_shift / (1.0 + (flow_shift - 1.0) * moment) ** 2


def pack_body(place, *refs):
    sources, outs = refs[:3], refs[3:]
    for number, out in enumerate(outs):

        @pl.when(pl.program_id(0) == number)
        def _(out=out):
            for kind, source in enumerate(sources):
                out[kind] = source[...]


def pack(place, sources, steps):
    tokens = sources[0].shape[0]

    def column(i, place):
        step = sum(jnp.where(i == n, step, 0) for n, step in enumerate(steps))
        return 0, (place[3] + step) % Z

    return pl.pallas_call(
        pack_body,
        grid_spec=pltpu.PrefetchScalarGridSpec(
            num_scalar_prefetch=1,
            grid=(len(steps),),
            in_specs=[pl.BlockSpec((tokens, HSIZE), column)] * len(sources),
            out_specs=[pl.BlockSpec((3, tokens, HSIZE), lambda i, place: (0, 0, 0))] * len(steps),
        ),
        out_shape=[jax.ShapeDtypeStruct((3, tokens, HSIZE), jnp.bfloat16)] * len(steps),
        compiler_params=pltpu.CompilerParams(vmem_limit_bytes=56 * 2**20),
    )(place, *sources)


def attend_body(*refs, heads, parts, chunk):
    query_refs, refs = refs[:heads], refs[heads:]
    key_refs, value_refs, refs = refs[:parts], refs[parts : 2 * parts], refs[2 * parts :]
    out_refs, (query_ref, keys_t, values_one) = refs[:heads], refs[heads:]
    tokens = values_one.shape[0]

    for index in range(heads):

        @pl.when(pl.program_id(0) == index)
        def _(ref=query_refs[index]):
            query_ref[...] = ref[...]

    @pl.when(pl.program_id(0) == 0)
    def _():
        step, start = 384, 0
        for key_ref, value_ref in zip(key_refs, value_refs):
            length = key_ref.shape[0]
            for at in range(0, length, step):
                block = key_ref[at : at + step, :].astype(jnp.float32).T.astype(jnp.bfloat16)
                keys_t[:HSIZE, start + at : start + at + step] = block
                keys_t[HSIZE:, start + at : start + at + step] = block
            values_one[start : start + length, :HSIZE] = value_ref[...]
            start += length
        values_one[:, HSIZE:] = jnp.ones((tokens, HSIZE), jnp.bfloat16)

    scaled = query_ref[...].astype(jnp.float32) * (math.log2(math.e) / math.sqrt(HSIZE))
    upper = scaled.astype(jnp.bfloat16)
    lower = (scaled - upper.astype(jnp.float32)).astype(jnp.bfloat16)
    queries = jnp.concatenate([upper, lower], axis=1)

    def score(at):
        return jnp.dot(queries, keys_t[:, at : at + chunk], preferred_element_type=jnp.float32)

    peak, total = None, None
    scores = score(0)
    for at in range(0, tokens, chunk):
        following = score(at + chunk) if at + chunk < tokens else None
        new_peak = jnp.max(scores, axis=1, keepdims=True)
        if at > 0:
            new_peak = jnp.maximum(peak, new_peak)
        weights = jnp.exp2(scores - new_peak).astype(jnp.bfloat16)
        summed = jnp.dot(
            weights, values_one[at : at + chunk, :], preferred_element_type=jnp.float32
        )
        total = summed if at == 0 else total * jnp.exp2(peak - new_peak) + summed
        peak, scores = new_peak, following
    result = (total[:, :HSIZE] / total[:, HSIZE:]).astype(jnp.bfloat16)
    for index in range(heads):

        @pl.when(pl.program_id(0) == index)
        def _(ref=out_refs[index]):
            ref[...] = result


def attend(queries, keys, values, chunk=3072):
    rows = queries[0][0].shape[-2]
    tokens = sum(part.shape[1] for part, _ in keys)
    operands = (*queries, *keys, *values)

    def block(array, index):
        if array.ndim == 2:
            return pl.BlockSpec((array.shape[0], HSIZE), lambda i: (0, index))
        return pl.BlockSpec((pl.squeezed, array.shape[1], HSIZE), lambda i: (index, 0, 0))

    return pl.pallas_call(
        functools.partial(attend_body, heads=len(queries), parts=len(keys), chunk=chunk),
        grid=(len(queries),),
        in_specs=[block(*operand) for operand in operands],
        out_specs=[pl.BlockSpec((rows, HSIZE), lambda i: (0, 0))] * len(queries),
        out_shape=[jax.ShapeDtypeStruct((rows, HSIZE), jnp.bfloat16)] * len(queries),
        scratch_shapes=[
            pltpu.VMEM((rows, HSIZE), jnp.bfloat16),
            pltpu.VMEM((2 * HSIZE, tokens), jnp.bfloat16),
            pltpu.VMEM((tokens, 2 * HSIZE), jnp.bfloat16),
        ],
        compiler_params=pltpu.CompilerParams(vmem_limit_bytes=56 * 2**20),
        cost_estimate=pl.CostEstimate(flops=1000, bytes_accessed=1000, transcendentals=0),
    )(*(array for array, _ in operands))


def project_body(place, *refs, steps):
    count = (2 * Z + 2) * len(steps)
    operands, own_weight, other_weight, outs = refs[:count], *refs[count:][:2], refs[count + 2 : -2]
    rows, weight = refs[-2:]
    share = rows.shape[0] // len(steps)
    depth = own_weight.shape[0]

    @pl.when(pl.program_id(0) == 0)
    def _():
        for number, ref in enumerate(operands):
            index, number = divmod(number, 2 * Z + 2)
            side, head = divmod(number, Z + 1)
            at = side * depth + (spread(place, head) if head < Z else Z * HSIZE)
            rows[index * share : (index + 1) * share, pl.ds(at, HSIZE)] = ref[...]

    weight[:depth] = own_weight[...]
    weight[depth:] = other_weight[...]
    product = jnp.dot(rows[...], weight[...], preferred_element_type=jnp.float32)
    height = outs[0].shape[0]
    for index, out in enumerate(outs):
        out[...] = product[index * height : (index + 1) * height].astype(out.dtype)


def spread(place, step):
    return pl.multiple_of((place[3] + step) % Z * HSIZE, HSIZE)


def project(place, attended, own_weight, other_weight, steps, kinds, height, tile=1280):
    depth, half = other_weight.shape
    share = attended[0].shape[0] // X
    rows, tiles = share * len(steps), half // tile
    return pl.pallas_call(
        functools.partial(project_body, steps=steps),
        grid_spec=pltpu.PrefetchScalarGridSpec(
            num_scalar_prefetch=1,
            grid=(tiles,),
            in_specs=[
                pl.BlockSpec((share, HSIZE), lambda i, place, step=step: ((place[0] + step) % X, 0))
                for step in steps
                for _ in attended
            ]
            + [
                pl.BlockSpec((depth, tile), lambda i, place: (0, place[1] * tiles + i)),
                pl.BlockSpec((depth, tile), lambda i, place: (0, i)),
            ],
            out_specs=[pl.BlockSpec((height, tile), lambda i, place: (0, i))] * len(kinds),
            scratch_shapes=[
                pltpu.VMEM((rows, 2 * depth), jnp.bfloat16),
                pltpu.VMEM((2 * depth, tile), jnp.bfloat16),
            ],
        ),
        out_shape=[jax.ShapeDtypeStruct((height, half), kind) for kind in kinds],
        compiler_params=pltpu.CompilerParams(vmem_limit_bytes=56 * 2**20),
        cost_estimate=pl.CostEstimate(flops=1000, bytes_accessed=1000, transcendentals=0),
    )(place, *(attended * len(steps)), own_weight, other_weight)


def finish_body(place, *refs):
    own, arrived, hidden, gate, scale, head_weight = refs[:2], refs[2:6], *refs[6:10]
    kept, given, total, turned = refs[10:]
    index = pl.program_id(0)
    summed = [
        own[n][...] + arrived[n][...].astype(jnp.float32) + arrived[2 + n][...].astype(jnp.float32)
        for n in range(2)
    ]
    residual = hidden[...].astype(jnp.float32) + gate[...] * jnp.concatenate(summed, axis=0)
    rest = residual * scale[...]
    projected = None
    for _ in range(3):
        part = rest.astype(jnp.bfloat16)
        rest = rest - part.astype(jnp.float32)
        product = jnp.dot(part, head_weight[...], preferred_element_type=jnp.float32)
        projected = product if projected is None else projected + product
    channels = projected.shape[1]
    plain = jnp.sum(residual, axis=1, keepdims=True)
    square = jnp.sum(residual * residual, axis=1, keepdims=True)
    lane = lax.broadcasted_iota(jnp.int32, (residual.shape[0], HSIZE - channels), 1)
    sums = jnp.where(lane == 0, plain, jnp.where(lane == 1, square, 0.0))
    parts = jnp.concatenate([projected, sums], axis=1)

    @pl.when(index == 0)
    def _():
        total[...] = parts

    @pl.when(index > 0)
    def _():
        total[...] += parts

    @pl.when(index == pl.num_programs(0) - 1)
    def _():
        turned[...] = total[...].T
        part = channels // 2
        for out, branch in ((kept, place[2]), (given, 1 - place[2])):
            out[:part] = turned[pl.ds(pl.multiple_of(branch * part, part), part), :]
            out[part:] = turned[channels : channels + out.shape[0] - part, :]


def finish(place, own, arrived, hidden, gate, scale, head_weight, tile=1280):
    middle, half = own[0].shape
    share, tiles = 2 * middle, half // tile
    height = head_weight.shape[1] // 2 + SUMS
    block = pl.BlockSpec((middle, tile), lambda i, place: (0, i))
    vector = pl.BlockSpec((1, tile), lambda i, place: (0, place[1] * tiles + i))
    return pl.pallas_call(
        finish_body,
        grid_spec=pltpu.PrefetchScalarGridSpec(
            num_scalar_prefetch=1,
            grid=(tiles,),
            in_specs=[block] * 6
            + [
                pl.BlockSpec((share, tile), lambda i, place: (place[0], place[1] * tiles + i)),
                vector,
                vector,
                pl.BlockSpec(
                    (tile, head_weight.shape[1]), lambda i, place: (place[1] * tiles + i, 0)
                ),
            ],
            out_specs=[pl.BlockSpec((height, share), lambda i, place: (0, 0))] * 2,
            scratch_shapes=[
                pltpu.VMEM((share, HSIZE), jnp.float32),
                pltpu.VMEM((HSIZE, share), jnp.float32),
            ],
        ),
        out_shape=[jax.ShapeDtypeStruct((height, share), jnp.float32)] * 2,
        compiler_params=pltpu.CompilerParams(vmem_limit_bytes=56 * 2**20),
        cost_estimate=pl.CostEstimate(
            flops=6 * share * half * HSIZE, bytes_accessed=12 * share * half, transcendentals=0
        ),
    )(place, *own, *arrived, hidden, gate[None], scale[None], head_weight)


def per_device(
    queries,
    keys,
    values,
    hidden_in,
    out_weight,
    gate,
    mod_scale,
    mod_shift,
    head_weight,
    latent,
    history,
    step_index,
):
    queries, keys, values, hidden = queries[0], keys[0], values[0], hidden_in[0]
    local_tokens = queries.shape[0]
    full_width = hidden.shape[1]
    half, share = full_width // CORE, local_tokens // X
    core = lax.axis_index("head") % CORE
    column = lax.axis_index("head") // CORE
    branch = lax.axis_index("cfg")

    z = lax.axis_index("seq") // YH
    place = jnp.stack([column, core, branch, z]).astype(jnp.int32)
    pair = "seq", "head"

    fifth = jnp.stack([keys[:, Z * HSIZE :], values[:, Z * HSIZE :]])
    fifth = lax.all_gather(fifth, "seq", axis=1, tiled=True)
    order = (1, 3, 2, 0)
    messages = pack(place, (queries, keys, values), order)
    messages, weight = lax.optimization_barrier((messages, out_weight))
    near = {
        step: lax.ppermute(message, pair, traded(step)) for step, message in zip(order, messages)
    }
    other_weight = lax.ppermute(
        lax.dynamic_slice_in_dim(weight, (1 - core) * half, half, 1), "head", core_swap
    )
    far = {step: lax.ppermute(near[step], "head", core_swap) for step in order}
    near, far, other_weight = lax.optimization_barrier((near, far, other_weight))
    dealt = attend(
        [(near[step], 0) for step in order],
        [(side[step], 1) for side in (near, far) for step in order],
        [(side[step], 2) for side in (near, far) for step in order],
    )
    fifth_queries, dealt = lax.optimization_barrier((queries, dealt))
    back = {
        step: lax.ppermute(result, pair, traded(-step)) for step, result in zip(order, dealt)
    }
    (fifth_out,) = attend([(fifth_queries, Z)], [(fifth, 0)], [(fifth, 1)])
    back, fifth_out = lax.optimization_barrier((back, fifth_out))
    own_attended = [back[step] for step in range(Z)] + [fifth_out]
    attended = (
        *own_attended,
        *(lax.ppermute(part, "head", core_swap) for part in own_attended),
    )

    wire, middle = jnp.bfloat16, share // 2
    weights = out_weight, other_weight
    opposite = project(place, attended, *weights, (2,), (wire,) * 2, middle)
    behind_far = lax.ppermute(opposite[0], "head", x_shift(1))
    ahead_far = lax.ppermute(opposite[1], "head", x_shift(3))
    attended, opposite = lax.optimization_barrier((attended, opposite))
    *rest, own_upper, own_lower = project(
        place, attended, *weights, (1, 3, 0), (jnp.float32, wire, wire) + (jnp.float32,) * 3, middle
    )
    forward, forward_lower, backward_upper, backward = rest
    behind_lower = lax.ppermute(forward_lower, "head", x_shift(1))
    ahead_upper = lax.ppermute(backward_upper, "head", x_shift(3))
    forward = (forward + behind_far.astype(jnp.float32)).astype(wire)
    backward = (backward + ahead_far.astype(jnp.float32)).astype(wire)
    behind_upper = lax.ppermute(forward, "head", x_shift(1))
    ahead_lower = lax.ppermute(backward, "head", x_shift(3))
    arrived = behind_upper, behind_lower, ahead_upper, ahead_lower

    kept, given = finish(
        place, (own_upper, own_lower), arrived, hidden, gate, mod_scale, head_weight
    )
    here = kept + lax.ppermute(kept, "head", core_swap)
    there = lax.ppermute(given, "cfg", cfg_swap) + lax.ppermute(
        given, ("cfg", "head"), both_swap
    )
    channels = head_weight.shape[1] // 2
    levels = jnp.dot(
        head_weight.astype(jnp.float32).T,
        jnp.stack([mod_scale, mod_shift], axis=1),
        precision=lax.Precision.HIGHEST,
    )
    levels = lax.dynamic_slice_in_dim(levels, branch * channels, channels, 0)

    def velocity(total):
        center = total[channels : channels + 1] / full_width
        inverse = lax.rsqrt(total[channels + 1 : channels + 2] / full_width - center * center + epsilon)
        return (total[:channels] - center * levels[:, :1]) * inverse + levels[:, 1:]

    conditioned = velocity(jnp.where(branch == 0, here, there))
    unconditioned = velocity(jnp.where(branch == 0, there, here))
    guided = unconditioned + guide_scale * (conditioned - unconditioned)
    ring = [guided] + [lax.ppermute(guided, "head", x_shift(X - ahead)) for ahead in range(1, X)]
    guided = lax.dynamic_slice_in_dim(
        jnp.concatenate(ring + ring[:-1], axis=1), (X - column) % X * share, local_tokens, 1
    ).T

    current_step = step_index[0]
    slopes = [sigma_slope(current_step - behind) for behind in range(4)]
    combined = (
        55.0 * slopes[0] * guided
        - 59.0 * slopes[1] * history[0]
        + 37.0 * slopes[2] * history[1]
        - 9.0 * slopes[3] * history[2]
    ) / 24.0
    advanced = latent - combined / STEPS
    return (guided, advanced)


def solution(mesh):
    placed = (
        P("cfg", "seq", "head"),
        P("cfg", "seq", "head"),
        P("cfg", "seq", "head"),
        P("cfg", "seq", None),
        P("head", None),
        P(),
        P(),
        P(),
        P(),
        P("seq", "cfg"),
        P(None, "seq", "cfg"),
        P(),
    )
    return jax.shard_map(
        per_device,
        mesh=mesh,
        in_specs=placed,
        out_specs=(P("seq", "cfg"), P("seq", "cfg")),
        check_vma=False,
    )
```

```python
import functools
import math

import jax
import jax.numpy as jnp
from jax import lax
from jax.experimental import pallas as pl
from jax.experimental.pallas import tpu as pltpu
from jax.sharding import PartitionSpec as P

HSIZE = 128
STEPS = 50
SUMS = 8

guide_scale = 5.0
flow_shift = 5.0
epsilon = 1e-06

Z, YH, X, CORE = 4, 2, 4, 2
SEQ, HEAD = Z * YH, X * CORE

z_groups = [[z * YH + y for z in range(Z)] for y in range(YH)]
core_swap = [(h, h ^ 1) for h in range(HEAD)]
cfg_swap = [(0, 1), (1, 0)]
both_swap = [(n, n ^ (HEAD + 1)) for n in range(2 * HEAD)]


def traded(step):
    return [
        ((z * YH + y) * HEAD + x * CORE + c, ((z + step) % Z * YH + c) * HEAD + x * CORE + y)
        for z in range(Z)
        for y in range(YH)
        for x in range(X)
        for c in range(CORE)
    ]


def x_shift(step):
    return [(x * CORE + c, (x + step) % X * CORE + c) for x in range(X) for c in range(CORE)]


def sigma_slope(step_number):
    moment = 1.0 - step_number.astype(jnp.float32) / STEPS
    return flow_shift / (1.0 + (flow_shift - 1.0) * moment) ** 2


def pack_body(place, *refs):
    sources, outs = refs[:3], refs[3:]
    for number, out in enumerate(outs):

        @pl.when(pl.program_id(0) == number)
        def _(out=out):
            for kind, source in enumerate(sources):
                out[kind] = source[...]


def pack(place, sources, steps):
    tokens = sources[0].shape[0]

    def column(i, place):
        step = sum(jnp.where(i == n, step, 0) for n, step in enumerate(steps))
        return 0, (place[3] + step) % Z

    return pl.pallas_call(
        pack_body,
        grid_spec=pltpu.PrefetchScalarGridSpec(
            num_scalar_prefetch=1,
            grid=(len(steps),),
            in_specs=[pl.BlockSpec((tokens, HSIZE), column)] * len(sources),
            out_specs=[pl.BlockSpec((3, tokens, HSIZE), lambda i, place: (0, 0, 0))] * len(steps),
        ),
        out_shape=[jax.ShapeDtypeStruct((3, tokens, HSIZE), jnp.bfloat16)] * len(steps),
        compiler_params=pltpu.CompilerParams(vmem_limit_bytes=56 * 2**20),
    )(place, *sources)


def attend_body(*refs, heads, parts, chunk):
    query_refs, refs = refs[:heads], refs[heads:]
    key_refs, value_refs, refs = refs[:parts], refs[parts : 2 * parts], refs[2 * parts :]
    out_refs, (query_ref, keys_t, values_one) = refs[:heads], refs[heads:]
    tokens = values_one.shape[0]

    for index in range(heads):

        @pl.when(pl.program_id(0) == index)
        def _(ref=query_refs[index]):
            query_ref[...] = ref[...]

    @pl.when(pl.program_id(0) == 0)
    def _():
        step, start = 384, 0
        for key_ref, value_ref in zip(key_refs, value_refs):
            length = key_ref.shape[0]
            for at in range(0, length, step):
                block = key_ref[at : at + step, :].astype(jnp.float32).T.astype(jnp.bfloat16)
                keys_t[:HSIZE, start + at : start + at + step] = block
                keys_t[HSIZE:, start + at : start + at + step] = block
            values_one[start : start + length, :HSIZE] = value_ref[...]
            start += length
        values_one[:, HSIZE:] = jnp.ones((tokens, HSIZE), jnp.bfloat16)

    scaled = query_ref[...].astype(jnp.float32) * (math.log2(math.e) / math.sqrt(HSIZE))
    upper = scaled.astype(jnp.bfloat16)
    lower = (scaled - upper.astype(jnp.float32)).astype(jnp.bfloat16)
    queries = jnp.concatenate([upper, lower], axis=1)

    def score(at):
        return jnp.dot(queries, keys_t[:, at : at + chunk], preferred_element_type=jnp.float32)

    peak, total = None, None
    scores = score(0)
    for at in range(0, tokens, chunk):
        following = score(at + chunk) if at + chunk < tokens else None
        new_peak = jnp.max(scores, axis=1, keepdims=True)
        if at > 0:
            new_peak = jnp.maximum(peak, new_peak)
        weights = jnp.exp2(scores - new_peak).astype(jnp.bfloat16)
        summed = jnp.dot(
            weights, values_one[at : at + chunk, :], preferred_element_type=jnp.float32
        )
        total = summed if at == 0 else total * jnp.exp2(peak - new_peak) + summed
        peak, scores = new_peak, following
    result = (total[:, :HSIZE] / total[:, HSIZE:]).astype(jnp.bfloat16)
    for index in range(heads):

        @pl.when(pl.program_id(0) == index)
        def _(ref=out_refs[index]):
            ref[...] = result


def attend(queries, keys, values, chunk=3072):
    rows = queries[0][0].shape[-2]
    tokens = sum(part.shape[1] for part, _ in keys)
    operands = (*queries, *keys, *values)

    def block(array, index):
        if array.ndim == 2:
            return pl.BlockSpec((array.shape[0], HSIZE), lambda i: (0, index))
        return pl.BlockSpec((pl.squeezed, array.shape[1], HSIZE), lambda i: (index, 0, 0))

    return pl.pallas_call(
        functools.partial(attend_body, heads=len(queries), parts=len(keys), chunk=chunk),
        grid=(len(queries),),
        in_specs=[block(*operand) for operand in operands],
        out_specs=[pl.BlockSpec((rows, HSIZE), lambda i: (0, 0))] * len(queries),
        out_shape=[jax.ShapeDtypeStruct((rows, HSIZE), jnp.bfloat16)] * len(queries),
        scratch_shapes=[
            pltpu.VMEM((rows, HSIZE), jnp.bfloat16),
            pltpu.VMEM((2 * HSIZE, tokens), jnp.bfloat16),
            pltpu.VMEM((tokens, 2 * HSIZE), jnp.bfloat16),
        ],
        compiler_params=pltpu.CompilerParams(vmem_limit_bytes=56 * 2**20),
        cost_estimate=pl.CostEstimate(flops=1000, bytes_accessed=1000, transcendentals=0),
    )(*(array for array, _ in operands))


def project_body(place, *refs, pieces):
    count = (2 * Z + 2) * pieces
    operands, own_weight, other_weight, outs = refs[:count], *refs[count:][:2], refs[count + 2 : -2]
    rows, weight = refs[-2:]
    share = rows.shape[0] // pieces
    depth = own_weight.shape[0]

    @pl.when(pl.program_id(0) == 0)
    def _():
        for number, ref in enumerate(operands):
            index, number = divmod(number, 2 * Z + 2)
            side, head = divmod(number, Z + 1)
            at = side * depth + (spread(place, head) if head < Z else Z * HSIZE)
            rows[index * share : (index + 1) * share, pl.ds(at, HSIZE)] = ref[...]

    weight[:depth] = own_weight[...]
    weight[depth:] = other_weight[...]
    product = jnp.dot(rows[...], weight[...], preferred_element_type=jnp.float32)
    height = outs[0].shape[0]
    for index, out in enumerate(outs):
        out[...] = product[index * height : (index + 1) * height].astype(out.dtype)


def spread(place, step):
    return pl.multiple_of((place[3] + step) % Z * HSIZE, HSIZE)


def project(place, attended, own_weight, other_weight, pieces, kinds, tile=1280):
    depth, half = other_weight.shape
    height = attended[0].shape[0] // X // 2
    rows, tiles = height * len(pieces), half // tile
    return pl.pallas_call(
        functools.partial(project_body, pieces=len(pieces)),
        grid_spec=pltpu.PrefetchScalarGridSpec(
            num_scalar_prefetch=1,
            grid=(tiles,),
            in_specs=[
                pl.BlockSpec(
                    (height, HSIZE),
                    lambda i, place, step=step, n=n: ((place[0] + step) % X * 2 + n, 0),
                )
                for step, n in pieces
                for _ in attended
            ]
            + [
                pl.BlockSpec((depth, tile), lambda i, place: (0, place[1] * tiles + i)),
                pl.BlockSpec((depth, tile), lambda i, place: (0, i)),
            ],
            out_specs=[pl.BlockSpec((height, tile), lambda i, place: (0, i))] * len(kinds),
            scratch_shapes=[
                pltpu.VMEM((rows, 2 * depth), jnp.bfloat16),
                pltpu.VMEM((2 * depth, tile), jnp.bfloat16),
            ],
        ),
        out_shape=[jax.ShapeDtypeStruct((height, half), kind) for kind in kinds],
        compiler_params=pltpu.CompilerParams(vmem_limit_bytes=56 * 2**20),
        cost_estimate=pl.CostEstimate(flops=1000, bytes_accessed=1000, transcendentals=0),
    )(place, *(attended * len(pieces)), own_weight, other_weight)


def finish_body(place, *refs):
    own, arrived, hidden, gate, scale, head_weight = refs[:2], refs[2:6], *refs[6:10]
    kept, given, total, turned = refs[10:]
    index = pl.program_id(0)
    summed = [
        own[n][...] + arrived[n][...].astype(jnp.float32) + arrived[2 + n][...].astype(jnp.float32)
        for n in range(2)
    ]
    residual = hidden[...].astype(jnp.float32) + gate[...] * jnp.concatenate(summed, axis=0)
    rest = residual * scale[...]
    projected = None
    for _ in range(3):
        part = rest.astype(jnp.bfloat16)
        rest = rest - part.astype(jnp.float32)
        product = jnp.dot(part, head_weight[...], preferred_element_type=jnp.float32)
        projected = product if projected is None else projected + product
    channels = projected.shape[1]
    plain = jnp.sum(residual, axis=1, keepdims=True)
    square = jnp.sum(residual * residual, axis=1, keepdims=True)
    lane = lax.broadcasted_iota(jnp.int32, (residual.shape[0], HSIZE - channels), 1)
    sums = jnp.where(lane == 0, plain, jnp.where(lane == 1, square, 0.0))
    parts = jnp.concatenate([projected, sums], axis=1)

    @pl.when(index == 0)
    def _():
        total[...] = parts

    @pl.when(index > 0)
    def _():
        total[...] += parts

    @pl.when(index == pl.num_programs(0) - 1)
    def _():
        turned[...] = total[...].T
        part = channels // 2
        for out, branch in ((kept, place[2]), (given, 1 - place[2])):
            out[:part] = turned[pl.ds(pl.multiple_of(branch * part, part), part), :]
            out[part:] = turned[channels : channels + out.shape[0] - part, :]


def finish(place, own, arrived, hidden, gate, scale, head_weight, tile=1280):
    middle, half = own[0].shape
    share, tiles = 2 * middle, half // tile
    height = head_weight.shape[1] // 2 + SUMS
    block = pl.BlockSpec((middle, tile), lambda i, place: (0, i))
    vector = pl.BlockSpec((1, tile), lambda i, place: (0, place[1] * tiles + i))
    return pl.pallas_call(
        finish_body,
        grid_spec=pltpu.PrefetchScalarGridSpec(
            num_scalar_prefetch=1,
            grid=(tiles,),
            in_specs=[block] * 6
            + [
                pl.BlockSpec((share, tile), lambda i, place: (place[0], place[1] * tiles + i)),
                vector,
                vector,
                pl.BlockSpec(
                    (tile, head_weight.shape[1]), lambda i, place: (place[1] * tiles + i, 0)
                ),
            ],
            out_specs=[pl.BlockSpec((height, share), lambda i, place: (0, 0))] * 2,
            scratch_shapes=[
                pltpu.VMEM((share, HSIZE), jnp.float32),
                pltpu.VMEM((HSIZE, share), jnp.float32),
            ],
        ),
        out_shape=[jax.ShapeDtypeStruct((height, share), jnp.float32)] * 2,
        compiler_params=pltpu.CompilerParams(vmem_limit_bytes=56 * 2**20),
        cost_estimate=pl.CostEstimate(
            flops=6 * share * half * HSIZE, bytes_accessed=12 * share * half, transcendentals=0
        ),
    )(place, *own, *arrived, hidden, gate[None], scale[None], head_weight)


def per_device(
    queries,
    keys,
    values,
    hidden_in,
    out_weight,
    gate,
    mod_scale,
    mod_shift,
    head_weight,
    latent,
    history,
    step_index,
):
    queries, keys, values, hidden = queries[0], keys[0], values[0], hidden_in[0]
    local_tokens = queries.shape[0]
    full_width = hidden.shape[1]
    half, share = full_width // CORE, local_tokens // X
    core = lax.axis_index("head") % CORE
    column = lax.axis_index("head") // CORE
    branch = lax.axis_index("cfg")

    z = lax.axis_index("seq") // YH
    place = jnp.stack([column, core, branch, z]).astype(jnp.int32)
    pair = "seq", "head"

    fifth = jnp.stack([keys[:, Z * HSIZE :], values[:, Z * HSIZE :]])
    fifth = lax.all_gather(fifth, "seq", axis=1, tiled=True)
    order = (1, 3, 2, 0)
    messages = pack(place, (queries, keys, values), order)
    messages, weight = lax.optimization_barrier((messages, out_weight))
    near = {
        step: lax.ppermute(message, pair, traded(step)) for step, message in zip(order, messages)
    }
    other_weight = lax.ppermute(
        lax.dynamic_slice_in_dim(weight, (1 - core) * half, half, 1), "head", core_swap
    )
    far = {step: lax.ppermute(near[step], "head", core_swap) for step in order}
    near, far, other_weight = lax.optimization_barrier((near, far, other_weight))
    dealt = attend(
        [(near[step], 0) for step in order],
        [(side[step], 1) for side in (near, far) for step in order],
        [(side[step], 2) for side in (near, far) for step in order],
    )
    fifth_queries, dealt = lax.optimization_barrier((queries, dealt))
    back = {
        step: lax.ppermute(result, pair, traded(-step)) for step, result in zip(order, dealt)
    }
    (fifth_out,) = attend([(fifth_queries, Z)], [(fifth, 0)], [(fifth, 1)])
    back, fifth_out = lax.optimization_barrier((back, fifth_out))
    own_attended = [back[step] for step in range(Z)] + [fifth_out]
    attended = (
        *own_attended,
        *(lax.ppermute(part, "head", core_swap) for part in own_attended),
    )

    wire = jnp.bfloat16
    weights = out_weight, other_weight
    opposite = project(place, attended, *weights, ((2, 0), (2, 1)), (wire,) * 2)
    behind_far = lax.ppermute(opposite[0], "head", x_shift(1))
    ahead_far = lax.ppermute(opposite[1], "head", x_shift(3))
    attended, opposite = lax.optimization_barrier((attended, opposite))
    forward_lower, backward_upper = project(
        place, attended, *weights, ((1, 1), (3, 0)), (wire,) * 2
    )
    behind_lower = lax.ppermute(forward_lower, "head", x_shift(1))
    ahead_upper = lax.ppermute(backward_upper, "head", x_shift(3))
    attended, forward_lower = lax.optimization_barrier((attended, forward_lower))
    forward, backward, own_upper, own_lower = project(
        place, attended, *weights, ((1, 0), (3, 1), (0, 0), (0, 1)), (jnp.float32,) * 4
    )
    forward = (forward + behind_far.astype(jnp.float32)).astype(wire)
    backward = (backward + ahead_far.astype(jnp.float32)).astype(wire)
    behind_upper = lax.ppermute(forward, "head", x_shift(1))
    ahead_lower = lax.ppermute(backward, "head", x_shift(3))
    arrived = behind_upper, behind_lower, ahead_upper, ahead_lower

    kept, given = finish(
        place, (own_upper, own_lower), arrived, hidden, gate, mod_scale, head_weight
    )
    here = kept + lax.ppermute(kept, "head", core_swap)
    there = lax.ppermute(given, "cfg", cfg_swap) + lax.ppermute(
        given, ("cfg", "head"), both_swap
    )
    channels = head_weight.shape[1] // 2
    levels = jnp.dot(
        head_weight.astype(jnp.float32).T,
        jnp.stack([mod_scale, mod_shift], axis=1),
        precision=lax.Precision.HIGHEST,
    )
    levels = lax.dynamic_slice_in_dim(levels, branch * channels, channels, 0)

    def velocity(total):
        center = total[channels : channels + 1] / full_width
        inverse = lax.rsqrt(total[channels + 1 : channels + 2] / full_width - center * center + epsilon)
        return (total[:channels] - center * levels[:, :1]) * inverse + levels[:, 1:]

    conditioned = velocity(jnp.where(branch == 0, here, there))
    unconditioned = velocity(jnp.where(branch == 0, there, here))
    guided = unconditioned + guide_scale * (conditioned - unconditioned)
    ring = [guided] + [lax.ppermute(guided, "head", x_shift(X - ahead)) for ahead in range(1, X)]
    guided = lax.dynamic_slice_in_dim(
        jnp.concatenate(ring + ring[:-1], axis=1), (X - column) % X * share, local_tokens, 1
    ).T

    current_step = step_index[0]
    slopes = [sigma_slope(current_step - behind) for behind in range(4)]
    combined = (
        55.0 * slopes[0] * guided
        - 59.0 * slopes[1] * history[0]
        + 37.0 * slopes[2] * history[1]
        - 9.0 * slopes[3] * history[2]
    ) / 24.0
    advanced = latent - combined / STEPS
    return (guided, advanced)


def solution(mesh):
    placed = (
        P("cfg", "seq", "head"),
        P("cfg", "seq", "head"),
        P("cfg", "seq", "head"),
        P("cfg", "seq", None),
        P("head", None),
        P(),
        P(),
        P(),
        P(),
        P("seq", "cfg"),
        P(None, "seq", "cfg"),
        P(),
    )
    return jax.shard_map(
        per_device,
        mesh=mesh,
        in_specs=placed,
        out_specs=(P("seq", "cfg"), P("seq", "cfg")),
        check_vma=False,
    )
```

```python
import functools
import math

import jax
import jax.numpy as jnp
from jax import lax
from jax.experimental import pallas as pl
from jax.experimental.pallas import tpu as pltpu
from jax.sharding import PartitionSpec as P

HSIZE = 128
STEPS = 50
SUMS = 8

guide_scale = 5.0
flow_shift = 5.0
epsilon = 1e-06

Z, YH, X, CORE = 4, 2, 4, 2
SEQ, HEAD = Z * YH, X * CORE

z_groups = [[z * YH + y for z in range(Z)] for y in range(YH)]
core_swap = [(h, h ^ 1) for h in range(HEAD)]
cfg_swap = [(0, 1), (1, 0)]
both_swap = [(n, n ^ (HEAD + 1)) for n in range(2 * HEAD)]


def traded(step):
    return [
        ((z * YH + y) * HEAD + x * CORE + c, ((z + step) % Z * YH + c) * HEAD + x * CORE + y)
        for z in range(Z)
        for y in range(YH)
        for x in range(X)
        for c in range(CORE)
    ]


def x_shift(step):
    return [(x * CORE + c, (x + step) % X * CORE + c) for x in range(X) for c in range(CORE)]


def sigma_slope(step_number):
    moment = 1.0 - step_number.astype(jnp.float32) / STEPS
    return flow_shift / (1.0 + (flow_shift - 1.0) * moment) ** 2


def pack_body(place, *refs):
    sources, outs = refs[:3], refs[3:]
    for number, out in enumerate(outs):

        @pl.when(pl.program_id(0) == number)
        def _(out=out):
            for kind, source in enumerate(sources):
                out[kind] = source[...]


def pack(place, sources, steps):
    tokens = sources[0].shape[0]

    def column(i, place):
        step = sum(jnp.where(i == n, step, 0) for n, step in enumerate(steps))
        return 0, (place[3] + step) % Z

    return pl.pallas_call(
        pack_body,
        grid_spec=pltpu.PrefetchScalarGridSpec(
            num_scalar_prefetch=1,
            grid=(len(steps),),
            in_specs=[pl.BlockSpec((tokens, HSIZE), column)] * len(sources),
            out_specs=[pl.BlockSpec((3, tokens, HSIZE), lambda i, place: (0, 0, 0))] * len(steps),
        ),
        out_shape=[jax.ShapeDtypeStruct((3, tokens, HSIZE), jnp.bfloat16)] * len(steps),
        compiler_params=pltpu.CompilerParams(vmem_limit_bytes=56 * 2**20),
    )(place, *sources)


def attend_body(*refs, heads, parts, chunk):
    query_refs, refs = refs[:heads], refs[heads:]
    key_refs, value_refs, refs = refs[:parts], refs[parts : 2 * parts], refs[2 * parts :]
    out_refs, (query_ref, keys_t, values_one) = refs[:heads], refs[heads:]
    tokens = values_one.shape[0]

    for index in range(heads):

        @pl.when(pl.program_id(0) == index)
        def _(ref=query_refs[index]):
            query_ref[...] = ref[...]

    @pl.when(pl.program_id(0) == 0)
    def _():
        step, start = 384, 0
        for key_ref, value_ref in zip(key_refs, value_refs):
            length = key_ref.shape[0]
            for at in range(0, length, step):
                block = key_ref[at : at + step, :].astype(jnp.float32).T.astype(jnp.bfloat16)
                keys_t[:HSIZE, start + at : start + at + step] = block
                keys_t[HSIZE:, start + at : start + at + step] = block
            values_one[start : start + length, :HSIZE] = value_ref[...]
            start += length
        values_one[:, HSIZE:] = jnp.ones((tokens, HSIZE), jnp.bfloat16)

    scaled = query_ref[...].astype(jnp.float32) * (math.log2(math.e) / math.sqrt(HSIZE))
    upper = scaled.astype(jnp.bfloat16)
    lower = (scaled - upper.astype(jnp.float32)).astype(jnp.bfloat16)
    queries = jnp.concatenate([upper, lower], axis=1)

    def score(at):
        return jnp.dot(queries, keys_t[:, at : at + chunk], preferred_element_type=jnp.float32)

    peak, total = None, None
    scores = score(0)
    for at in range(0, tokens, chunk):
        following = score(at + chunk) if at + chunk < tokens else None
        new_peak = jnp.max(scores, axis=1, keepdims=True)
        if at > 0:
            new_peak = jnp.maximum(peak, new_peak)
        weights = jnp.exp2(scores - new_peak).astype(jnp.bfloat16)
        summed = jnp.dot(
            weights, values_one[at : at + chunk, :], preferred_element_type=jnp.float32
        )
        total = summed if at == 0 else total * jnp.exp2(peak - new_peak) + summed
        peak, scores = new_peak, following
    result = (total[:, :HSIZE] / total[:, HSIZE:]).astype(jnp.bfloat16)
    for index in range(heads):

        @pl.when(pl.program_id(0) == index)
        def _(ref=out_refs[index]):
            ref[...] = result


def attend(queries, keys, values, chunk=3072):
    rows = queries[0][0].shape[-2]
    tokens = sum(part.shape[1] for part, _ in keys)
    operands = (*queries, *keys, *values)

    def block(array, index):
        if array.ndim == 2:
            return pl.BlockSpec((array.shape[0], HSIZE), lambda i: (0, index))
        return pl.BlockSpec((pl.squeezed, array.shape[1], HSIZE), lambda i: (index, 0, 0))

    return pl.pallas_call(
        functools.partial(attend_body, heads=len(queries), parts=len(keys), chunk=chunk),
        grid=(len(queries),),
        in_specs=[block(*operand) for operand in operands],
        out_specs=[pl.BlockSpec((rows, HSIZE), lambda i: (0, 0))] * len(queries),
        out_shape=[jax.ShapeDtypeStruct((rows, HSIZE), jnp.bfloat16)] * len(queries),
        scratch_shapes=[
            pltpu.VMEM((rows, HSIZE), jnp.bfloat16),
            pltpu.VMEM((2 * HSIZE, tokens), jnp.bfloat16),
            pltpu.VMEM((tokens, 2 * HSIZE), jnp.bfloat16),
        ],
        compiler_params=pltpu.CompilerParams(vmem_limit_bytes=56 * 2**20),
        cost_estimate=pl.CostEstimate(flops=1000, bytes_accessed=1000, transcendentals=0),
    )(*(array for array, _ in operands))


def project_body(place, *refs, pieces):
    count = (2 * Z + 2) * pieces
    operands, own_weight, other_weight, outs = refs[:count], *refs[count:][:2], refs[count + 2 : -2]
    rows, weight = refs[-2:]
    share = rows.shape[0] // pieces
    depth = own_weight.shape[0]

    @pl.when(pl.program_id(0) == 0)
    def _():
        for number, ref in enumerate(operands):
            index, number = divmod(number, 2 * Z + 2)
            side, head = divmod(number, Z + 1)
            at = side * depth + (spread(place, head) if head < Z else Z * HSIZE)
            rows[index * share : (index + 1) * share, pl.ds(at, HSIZE)] = ref[...]

    weight[:depth] = own_weight[...]
    weight[depth:] = other_weight[...]
    product = jnp.dot(rows[...], weight[...], preferred_element_type=jnp.float32)
    height = outs[0].shape[0]
    for index, out in enumerate(outs):
        out[...] = product[index * height : (index + 1) * height].astype(out.dtype)


def spread(place, step):
    return pl.multiple_of((place[3] + step) % Z * HSIZE, HSIZE)


def project(place, attended, own_weight, other_weight, pieces, kinds, tile=1280):
    depth, half = other_weight.shape
    height = attended[0].shape[0] // X // 2
    rows, tiles = height * len(pieces), half // tile
    return pl.pallas_call(
        functools.partial(project_body, pieces=len(pieces)),
        grid_spec=pltpu.PrefetchScalarGridSpec(
            num_scalar_prefetch=1,
            grid=(tiles,),
            in_specs=[
                pl.BlockSpec(
                    (height, HSIZE),
                    lambda i, place, step=step, n=n: ((place[0] + step) % X * 2 + n, 0),
                )
                for step, n in pieces
                for _ in attended
            ]
            + [
                pl.BlockSpec((depth, tile), lambda i, place: (0, place[1] * tiles + i)),
                pl.BlockSpec((depth, tile), lambda i, place: (0, i)),
            ],
            out_specs=[pl.BlockSpec((height, tile), lambda i, place: (0, i))] * len(kinds),
            scratch_shapes=[
                pltpu.VMEM((rows, 2 * depth), jnp.bfloat16),
                pltpu.VMEM((2 * depth, tile), jnp.bfloat16),
            ],
        ),
        out_shape=[jax.ShapeDtypeStruct((height, half), kind) for kind in kinds],
        compiler_params=pltpu.CompilerParams(vmem_limit_bytes=56 * 2**20),
        cost_estimate=pl.CostEstimate(flops=1000, bytes_accessed=1000, transcendentals=0),
    )(place, *(attended * len(pieces)), own_weight, other_weight)


def finish_body(place, *refs):
    own, arrived, hidden, gate, scale, head_weight = refs[:2], refs[2:6], *refs[6:10]
    kept, given, total, turned = refs[10:]
    index = pl.program_id(0)
    summed = [
        own[n][...] + arrived[n][...].astype(jnp.float32) + arrived[2 + n][...].astype(jnp.float32)
        for n in range(2)
    ]
    residual = hidden[...].astype(jnp.float32) + gate[...] * jnp.concatenate(summed, axis=0)
    rest = residual * scale[...]
    projected = None
    for _ in range(3):
        part = rest.astype(jnp.bfloat16)
        rest = rest - part.astype(jnp.float32)
        product = jnp.dot(part, head_weight[...], preferred_element_type=jnp.float32)
        projected = product if projected is None else projected + product
    channels = projected.shape[1]
    plain = jnp.sum(residual, axis=1, keepdims=True)
    square = jnp.sum(residual * residual, axis=1, keepdims=True)
    lane = lax.broadcasted_iota(jnp.int32, (residual.shape[0], HSIZE - channels), 1)
    sums = jnp.where(lane == 0, plain, jnp.where(lane == 1, square, 0.0))
    parts = jnp.concatenate([projected, sums], axis=1)

    @pl.when(index == 0)
    def _():
        total[...] = parts

    @pl.when(index > 0)
    def _():
        total[...] += parts

    @pl.when(index == pl.num_programs(0) - 1)
    def _():
        turned[...] = total[...].T
        part = channels // 2
        for out, branch in ((kept, place[2]), (given, 1 - place[2])):
            out[:part] = turned[pl.ds(pl.multiple_of(branch * part, part), part), :]
            out[part:] = turned[channels : channels + out.shape[0] - part, :]


def finish(place, own, arrived, hidden, gate, scale, head_weight, tile=1280):
    middle, half = own[0].shape
    share, tiles = 2 * middle, half // tile
    height = head_weight.shape[1] // 2 + SUMS
    block = pl.BlockSpec((middle, tile), lambda i, place: (0, i))
    vector = pl.BlockSpec((1, tile), lambda i, place: (0, place[1] * tiles + i))
    return pl.pallas_call(
        finish_body,
        grid_spec=pltpu.PrefetchScalarGridSpec(
            num_scalar_prefetch=1,
            grid=(tiles,),
            in_specs=[block] * 6
            + [
                pl.BlockSpec((share, tile), lambda i, place: (place[0], place[1] * tiles + i)),
                vector,
                vector,
                pl.BlockSpec(
                    (tile, head_weight.shape[1]), lambda i, place: (place[1] * tiles + i, 0)
                ),
            ],
            out_specs=[pl.BlockSpec((height, share), lambda i, place: (0, 0))] * 2,
            scratch_shapes=[
                pltpu.VMEM((share, HSIZE), jnp.float32),
                pltpu.VMEM((HSIZE, share), jnp.float32),
            ],
        ),
        out_shape=[jax.ShapeDtypeStruct((height, share), jnp.float32)] * 2,
        compiler_params=pltpu.CompilerParams(vmem_limit_bytes=56 * 2**20),
        cost_estimate=pl.CostEstimate(
            flops=6 * share * half * HSIZE, bytes_accessed=12 * share * half, transcendentals=0
        ),
    )(place, *own, *arrived, hidden, gate[None], scale[None], head_weight)


def per_device(
    queries,
    keys,
    values,
    hidden_in,
    out_weight,
    gate,
    mod_scale,
    mod_shift,
    head_weight,
    latent,
    history,
    step_index,
):
    queries, keys, values, hidden = queries[0], keys[0], values[0], hidden_in[0]
    local_tokens = queries.shape[0]
    full_width = hidden.shape[1]
    half, share = full_width // CORE, local_tokens // X
    core = lax.axis_index("head") % CORE
    column = lax.axis_index("head") // CORE
    branch = lax.axis_index("cfg")

    z = lax.axis_index("seq") // YH
    place = jnp.stack([column, core, branch, z]).astype(jnp.int32)
    pair = "seq", "head"

    fifth = jnp.stack([keys[:, Z * HSIZE :], values[:, Z * HSIZE :]])
    fifth = lax.all_gather(fifth, "seq", axis=1, tiled=True)
    order = (1, 3, 2, 0)
    messages = pack(place, (queries, keys, values), order)
    messages, weight = lax.optimization_barrier((messages, out_weight))
    near = {
        step: lax.ppermute(message, pair, traded(step)) for step, message in zip(order, messages)
    }
    other_weight = lax.ppermute(
        lax.dynamic_slice_in_dim(weight, (1 - core) * half, half, 1), "head", core_swap
    )
    far = {step: lax.ppermute(near[step], "head", core_swap) for step in order}
    near, far, other_weight = lax.optimization_barrier((near, far, other_weight))
    dealt = attend(
        [(near[step], 0) for step in order],
        [(side[step], 1) for side in (near, far) for step in order],
        [(side[step], 2) for side in (near, far) for step in order],
    )
    fifth_queries, dealt = lax.optimization_barrier((queries, dealt))
    back = {
        step: lax.ppermute(result, pair, traded(-step)) for step, result in zip(order, dealt)
    }
    (fifth_out,) = attend([(fifth_queries, Z)], [(fifth, 0)], [(fifth, 1)], chunk=1536)
    back, fifth_out = lax.optimization_barrier((back, fifth_out))
    own_attended = [back[step] for step in range(Z)] + [fifth_out]
    attended = (
        *own_attended,
        *(lax.ppermute(part, "head", core_swap) for part in own_attended),
    )

    wire = jnp.bfloat16
    weights = out_weight, other_weight
    opposite = project(place, attended, *weights, ((2, 0), (2, 1)), (wire,) * 2)
    behind_far = lax.ppermute(opposite[0], "head", x_shift(1))
    ahead_far = lax.ppermute(opposite[1], "head", x_shift(3))
    attended, opposite = lax.optimization_barrier((attended, opposite))
    forward_lower, backward_upper = project(
        place, attended, *weights, ((1, 1), (3, 0)), (wire,) * 2
    )
    behind_lower = lax.ppermute(forward_lower, "head", x_shift(1))
    ahead_upper = lax.ppermute(backward_upper, "head", x_shift(3))
    attended, forward_lower = lax.optimization_barrier((attended, forward_lower))
    forward, backward, own_upper, own_lower = project(
        place, attended, *weights, ((1, 0), (3, 1), (0, 0), (0, 1)), (jnp.float32,) * 4
    )
    forward = (forward + behind_far.astype(jnp.float32)).astype(wire)
    backward = (backward + ahead_far.astype(jnp.float32)).astype(wire)
    behind_upper = lax.ppermute(forward, "head", x_shift(1))
    ahead_lower = lax.ppermute(backward, "head", x_shift(3))
    arrived = behind_upper, behind_lower, ahead_upper, ahead_lower

    kept, given = finish(
        place, (own_upper, own_lower), arrived, hidden, gate, mod_scale, head_weight
    )
    here = kept + lax.ppermute(kept, "head", core_swap)
    there = lax.ppermute(given, "cfg", cfg_swap) + lax.ppermute(
        given, ("cfg", "head"), both_swap
    )
    channels = head_weight.shape[1] // 2
    levels = jnp.dot(
        head_weight.astype(jnp.float32).T,
        jnp.stack([mod_scale, mod_shift], axis=1),
        precision=lax.Precision.HIGHEST,
    )
    levels = lax.dynamic_slice_in_dim(levels, branch * channels, channels, 0)

    def velocity(total):
        center = total[channels : channels + 1] / full_width
        inverse = lax.rsqrt(total[channels + 1 : channels + 2] / full_width - center * center + epsilon)
        return (total[:channels] - center * levels[:, :1]) * inverse + levels[:, 1:]

    conditioned = velocity(jnp.where(branch == 0, here, there))
    unconditioned = velocity(jnp.where(branch == 0, there, here))
    guided = unconditioned + guide_scale * (conditioned - unconditioned)
    ring = [guided] + [lax.ppermute(guided, "head", x_shift(X - ahead)) for ahead in range(1, X)]
    guided = lax.dynamic_slice_in_dim(
        jnp.concatenate(ring + ring[:-1], axis=1), (X - column) % X * share, local_tokens, 1
    ).T

    current_step = step_index[0]
    slopes = [sigma_slope(current_step - behind) for behind in range(4)]
    combined = (
        55.0 * slopes[0] * guided
        - 59.0 * slopes[1] * history[0]
        + 37.0 * slopes[2] * history[1]
        - 9.0 * slopes[3] * history[2]
    ) / 24.0
    advanced = latent - combined / STEPS
    return (guided, advanced)


def solution(mesh):
    placed = (
        P("cfg", "seq", "head"),
        P("cfg", "seq", "head"),
        P("cfg", "seq", "head"),
        P("cfg", "seq", None),
        P("head", None),
        P(),
        P(),
        P(),
        P(),
        P("seq", "cfg"),
        P(None, "seq", "cfg"),
        P(),
    )
    return jax.shard_map(
        per_device,
        mesh=mesh,
        in_specs=placed,
        out_specs=(P("seq", "cfg"), P("seq", "cfg")),
        check_vma=False,
    )
```
